256 devices in a mesh: plane: 4 (over x_lo, core), sub: 64 (over x_hi, z, y).
Axes of the slice: x: 4 (x_hi: 2, x_lo: 2; x = x_hi * 2 + x_lo), y: 4, z: 8, core: 2. Of those that a mesh axis runs over, the one named last changes fastest.
Arguments:
- residual_in: bfloat16 [512, 128, 768], P(('plane', 'sub')), may hold values from -6 to 6
- schur: bfloat16 [512, 768, 768], P(('plane', 'sub')), may hold values from -0.21875 to 0.21875
- face_inverse: bfloat16 [512, 3, 256, 256], P(('plane', 'sub')), may hold values from -0.25 to 0.25
- local_inverse: bfloat16 [512, 768, 768], P(('plane', 'sub')), may hold values from -0.21875 to 0.21875
- basis: bfloat16 [512, 48, 768], P(('plane', 'sub')), may hold values from -0.21875 to 0.21875
- face_dofs: int32 [512, 768], P(('plane', 'sub')), may hold values from 0 to 767, each once within a row
- prim_map: int32 [512, 48], P(('plane', 'sub')), may hold values from 0 to 6143
- coarse_inverse: float32 [6144, 6144], P('sub'), as said below
Outputs:
- preconditioned: float32 [512, 128, 768], P(('plane', 'sub'))
The draws below stay inside these ranges and needn't reach their ends.
Inputs may be any that keep to these rules, and one draw needn't show every extreme that they name: `face_dofs`: each row is a permutation of the interface dofs. `coarse_inverse`: symmetric, with diagonal entries of order one.
All inputs are finite; a program needn't handle non-finite values.
Results may differ from the reference program's by a relative error of at most 0.015.
Values may be sent and summed in bfloat16 or wider, within the bound.
A program may use at most 64 MiB of HBM per device.

```python
import math
import jax
import jax.numpy as jnp
import numpy as np
from jax import lax

FACE = 256
NF = 3
IFACE = 768
RHS = 128
PRIM = 48
NC = 6144
SUBS = 512
N_PLANE = 4
N_SUB = 64


def draw_coarse_inverse(key, part):
    key = jax.random.fold_in(key, 7)
    first, second = jax.random.split(key)
    noise = jax.random.normal(first, (NC, NC), jnp.float32)
    symmetric = (noise + noise.T) * (0.35 / math.sqrt(NC))
    diagonal = jax.random.uniform(second, (NC,), jnp.float32, 0.5, 1.5)
    return symmetric + jnp.diag(diagonal)


def set_ends(entries, key, smallest, top_value):
    index_at = [jax.random.randint(jax.random.fold_in(key, axis), (), 0, length) for axis, length in enumerate(entries.shape)]
    longest = entries.shape.index(max(entries.shape))
    next_to = index_at[:longest] + [(index_at[longest] + 1) % entries.shape[longest]] + index_at[longest + 1:]
    return entries.at[tuple(index_at)].set(smallest).at[tuple(next_to)].set(top_value)


def block_scale(stream_key, shape, cuts, low, largest):
    def one(axis_at, blocks):
        heights = jax.random.uniform(jax.random.fold_in(jax.random.fold_in(stream_key, 6), axis_at), (blocks,), jnp.float32, low / len(cuts), largest / len(cuts))
        return jnp.repeat(jnp.exp(heights), shape[axis_at] // blocks).reshape((-1,) + (1,) * (len(shape) - axis_at - 1))

    gain = one(*cuts[0])
    for cut in cuts[1:]:
        gain = gain * one(*cut)
    return gain


def centred(key, dims, width, most, cuts=(), dtype=jnp.bfloat16):
    drawn = width * jax.random.normal(key, dims, jnp.float32)
    if cuts:
        drawn = drawn * block_scale(key, dims, cuts, -0.22, 0.18)
    return jnp.clip(drawn, -most, most).astype(dtype)


def setup_inputs(seed: int = 0) -> dict:
    arg_keys = jax.random.split(jax.random.key(seed), 9)
    residual_in = centred(arg_keys[0], (SUBS, RHS, IFACE), 1.0, 6.0, ((0, 256),))
    schur = centred(arg_keys[1], (SUBS, IFACE, IFACE), IFACE ** -0.5, 0.21875, ((0, 256),))
    face_inverse = centred(arg_keys[2], (SUBS, NF, FACE, FACE), (2 * FACE) ** -0.5, 0.25, ((0, 256),))
    local_inverse = centred(arg_keys[3], (SUBS, IFACE, IFACE), IFACE ** -0.5, 0.21875, ((0, 256),))
    basis = centred(arg_keys[4], (SUBS, PRIM, IFACE), IFACE ** -0.5, 0.21875, ((0, 256),))
    face_dofs = jax.vmap(lambda own: jax.random.permutation(own, IFACE))(jax.random.split(arg_keys[5], SUBS)).reshape((SUBS, IFACE)).astype(jnp.int32)
    prim_map = set_ends(jax.random.randint(arg_keys[6], (SUBS, PRIM), 0, NC), jax.random.fold_in(arg_keys[6], 1), 0, NC - 1).astype(jnp.int32)
    coarse_inverse = draw_coarse_inverse(jax.random.fold_in(arg_keys[8], 71), 0)
    return {"residual_in": residual_in, "schur": schur, "face_inverse": face_inverse, "local_inverse": local_inverse, "basis": basis, "face_dofs": face_dofs, "prim_map": prim_map, "coarse_inverse": coarse_inverse}


def local_terms(pieces):
    vector, schur, face_inverse, face_dofs = pieces
    image = jnp.dot(vector, schur.T, preferred_element_type=jnp.float32).astype(jnp.bfloat16)
    faces = image[:, face_dofs].reshape(RHS, NF, FACE)
    weighted = jnp.einsum('fqp,rfp->rfq', face_inverse.astype(jnp.float32), faces.astype(jnp.float32))
    return weighted.astype(jnp.bfloat16)


def deluxe(vector, schur, face_inverse, face_dofs):
    weighted = lax.map(local_terms, (vector, schur, face_inverse, face_dofs))
    grid = weighted.reshape(N_PLANE, N_SUB, 2, RHS, NF, FACE)
    same_chip = grid[:, :, ::-1, :, 0]
    cycle_first = jnp.roll(grid[:, :, 1, :, 1], 1, axis=1)
    cycle_second = jnp.roll(grid[:, :, 0, :, 1], -1, axis=1)
    cycle_partner = jnp.stack([cycle_first, cycle_second], axis=2)
    plane_first = grid[np.arange(N_PLANE) ^ 1][:, :, 0, :, 2]
    plane_second = grid[np.arange(N_PLANE) ^ 2][:, :, 1, :, 2]
    plane_partner = jnp.stack([plane_first, plane_second], axis=2)
    partner = jnp.stack([same_chip, cycle_partner, plane_partner], axis=4)
    summed = grid.astype(jnp.float32) + partner.astype(jnp.float32)
    summed = summed.reshape(SUBS, RHS, IFACE)
    order = jnp.argsort(face_dofs, axis=1).astype(jnp.int32)
    return jnp.take_along_axis(summed, order[:, None, :], axis=2)


def apply_local(pieces):
    return jnp.dot(pieces[0], pieces[1].T, preferred_element_type=jnp.float32)


def reference(residual_in, schur, face_inverse, local_inverse, basis, face_dofs, prim_map, coarse_inverse):
    averaged = deluxe(residual_in, schur, face_inverse, face_dofs).astype(jnp.bfloat16)
    local_part = lax.map(apply_local, (averaged, local_inverse))
    primal = lax.map(apply_local, (averaged, basis))
    flat = jnp.transpose(primal, (1, 0, 2)).reshape(RHS, SUBS * PRIM)
    coarse_residual = jnp.zeros((RHS, NC), jnp.float32).at[:, prim_map.reshape(-1)].add(flat)
    coarse_solution = jnp.dot(coarse_residual, coarse_inverse.T, precision=lax.Precision.HIGHEST)
    looked = jnp.transpose(coarse_solution[:, prim_map], (1, 0, 2))
    correction = jnp.einsum('nrm,nmi->nri', looked, basis.astype(jnp.float32), precision=lax.Precision.HIGHEST)
    corrected = (local_part + correction).astype(jnp.bfloat16)
    return deluxe(corrected, schur, face_inverse, face_dofs)
```

```python
import jax
import jax.numpy as jnp
from jax import lax
from jax.experimental import pallas as pl
from jax.experimental.pallas import tpu as pltpu
from jax.sharding import PartitionSpec as P

MESH = pl.DeviceIdType.MESH
F32, BF16, I32 = jnp.float32, jnp.bfloat16, jnp.int32
RHS, IFACE, FACE, PRIM = 128, 768, 256, 48
BOTH = 2 * PRIM
QUARTER = 1536
OWNERS = 32
PIECE = QUARTER // OWNERS


def mm(a, b):
    return jnp.dot(a, b, preferred_element_type=F32)


def onehot(mask):
    return jnp.where(mask, 1.0, 0.0).astype(BF16)


def column(row):
    return jnp.broadcast_to(row, (128, 128)).T


def kernel(
    res_h, schur_h, finv_h, linv_h, basis_h, fd_h, pm_h, cinv_h, out_h,
    res, schur, finv, linv, basis, fd, pm, cinv,
    pt, pp, img, vec, w, got, both, avg, loc, bpad, bt,
    pm_row, pm_all, con, oh1, oh2, rpart, rs, ag1, part, pr, ag2, lp, lr, looked, outv,
    load_sem, out_sem, face_send, face_recv, pm_send, pm_recv, con_send, con_recv,
    rs_send, rs_recv, ag1_send, ag1_recv, pr_send, pr_recv, ag2_send, ag2_recv, lk_send, lk_recv,
):
    p, s = lax.axis_index("plane"), lax.axis_index("sub")
    x, z, y = lax.div(s, 32), lax.rem(lax.div(s, 4), 8), lax.rem(s, 4)
    h, zm = lax.div(z, 4), lax.rem(z, 4)
    mine = zm * 8 + x * 4 + y

    def at(ax, az, ay):
        return lax.rem(ax, 2) * 32 + lax.rem(az, 8) * 4 + lax.rem(ay, 4)

    def ahead(j):
        step = lax.rem(lax.rem(lax.div(j, 4), 4) + 1, 4)
        return p, at(x + lax.div(j, 16), z + 7 + step, y + lax.rem(j, 4))

    def behind(j):
        step = lax.rem(lax.rem(lax.div(j, 4), 4) + 1, 4)
        return p, at(x + lax.div(j, 16), z + 9 - step, y + lax.rem(j, 4))

    def near(j):
        return lax.rem(p + lax.rem(j, 4), 4), at(x, z + 4 * lax.div(j, 4), y)

    up, down = lax.rem(s + 1, 64), lax.rem(s + 63, 64)
    core = p + 1 - 2 * lax.rem(p, 2)
    far = p + 2 - 4 * lax.div(p, 2)

    def load(i, src, dst):
        return pltpu.make_async_copy(src, dst, load_sem.at[i])

    loads = [
        load(0, fd_h, fd),
        load(1, pm_h, pm),
        load(2, res_h, res),
        load(3, schur_h.at[0], schur.at[0]),
        load(4, schur_h.at[1], schur.at[1]),
        load(5, finv_h, finv),
        load(6, basis_h, basis),
        load(7, linv_h, linv),
        load(8, cinv_h.at[:, pl.ds(pl.multiple_of(p * QUARTER, QUARTER), QUARTER)], cinv),
    ]
    for one in loads:
        one.start()

    con[...] = jnp.zeros_like(con)
    looked[...] = jnp.zeros_like(looked)
    barrier = pltpu.get_barrier_semaphore()

    def greet(to):
        pl.semaphore_signal(barrier, inc=1, device_id=to, device_id_type=MESH)

    def greet_behind(j, _):
        greet(behind(j))
        return 0

    def greet_near(j, _):
        greet(near(j))
        return 0

    lax.fori_loop(1, OWNERS, greet_behind, 0)
    lax.fori_loop(1, 8, greet_near, 0)
    greet((p, up))
    greet((p, down))

    loads[0].wait()
    for l in range(2):
        row = fd[l : l + 1, :].astype(F32)
        for m in range(3):
            rows = lax.broadcasted_iota(I32, (FACE, IFACE), 0).astype(F32) + float(m * FACE)
            pt[l, m * FACE : (m + 1) * FACE, :] = onehot(rows == row)
        for b in range(6):
            col = column(row[:, b * 128 : (b + 1) * 128])
            for c in range(6):
                lanes = lax.broadcasted_iota(I32, (128, 128), 1).astype(F32) + float(c * 128)
                pp[l, b * 128 : (b + 1) * 128, c * 128 : (c + 1) * 128] = onehot(col == lanes)

    loads[1].wait()
    pm_row[...] = jnp.full((8, 128), -1, I32)
    pm_row[0:2, 0:PRIM] = pm[...]
    first = pm_row[0:1, :]
    second = pltpu.roll(jnp.broadcast_to(pm_row[1:2, :], (8, 128)), PRIM, 1)
    lane = lax.broadcasted_iota(I32, (8, 128), 1)
    pm_row[...] = jnp.where(lane < PRIM, jnp.broadcast_to(first, (8, 128)), jnp.where(lane < BOTH, second, -1))
    slot = h * 4 + p
    pm_all[slot] = pm_row[...]

    def image(l, vector, transposed):
        for m in range(3):
            rows = schur[l, m * FACE : (m + 1) * FACE, :]
            if transposed:
                part_ = mm(rows, vector)
            else:
                part_ = lax.dot_general(rows, vector, (((1,), (1,)), ((), ())), preferred_element_type=F32)
            img[l, m * FACE : (m + 1) * FACE, :] = part_.astype(BF16)

    def weigh(d, l, k):
        faces = mm(pp[l, k * FACE : (k + 1) * FACE, :], img[l]).astype(BF16)
        w[d, l, k] = mm(finv[l, k], faces).astype(BF16)

    def face_copy(d, l, k):
        if k == 1:
            to, there = (p, down if l == 0 else up), 1 - l
        else:
            to, there = (core if l == 0 else far, s), 2 + l
        here = 2 * (k - 1) + l
        return pltpu.make_async_remote_copy(
            src_ref=w.at[d, l, k],
            dst_ref=got.at[d, there],
            send_sem=face_send.at[d, here],
            recv_sem=face_recv.at[d, there],
            device_id=to,
            device_id_type=MESH,
        )

    def arrived(d, slot_):
        pltpu.make_async_copy(got.at[d, slot_], got.at[d, slot_], face_recv.at[d, slot_]).wait()

    face_copies = []

    def exchange(d, vectors, transposed):
        for l in range(2):
            image(l, vectors[l], transposed)
            for k in (1, 2):
                weigh(d, l, k)
                if d == 0 and l == 0 and k == 1:
                    pl.semaphore_wait(barrier, OWNERS - 1 + 7 + 2)
                    lax.fori_loop(1, 8, send_pm, 0)
                one = face_copy(d, l, k)
                one.start()
                face_copies.append(one)
        for l in range(2):
            weigh(d, l, 0)

    def send_pm(j, _):
        pltpu.make_async_remote_copy(
            src_ref=pm_row, dst_ref=pm_all.at[slot], send_sem=pm_send, recv_sem=pm_recv,
            device_id=near(j), device_id_type=MESH,
        ).start()
        return 0

    loads[2].wait()
    loads[3].wait()
    loads[4].wait()
    loads[5].wait()
    exchange(0, [res[0], res[1]], False)

    loads[6].wait()
    bpad[...] = jnp.zeros_like(bpad)
    for l in range(2):
        bpad[l, l * PRIM : (l + 1) * PRIM, :] = basis[l].astype(F32)
        for b in range(6):
            bt[l, b * 128 : (b + 1) * 128, :] = bpad[l, :, b * 128 : (b + 1) * 128].T.astype(BF16)
    pltpu.make_async_copy(pm_all.at[pl.ds(0, 7)], pm_all.at[pl.ds(0, 7)], pm_recv).wait()
    for t in range(8):
        row = pm_all[t, 0:1, :].astype(F32) - (p * QUARTER).astype(F32)
        for m in range(6):
            rows = lax.broadcasted_iota(I32, (256, 128), 0).astype(F32) + float(m * 256)
            oh1[m * 256 : (m + 1) * 256, t * 128 : (t + 1) * 128] = onehot(rows == row)

    for l in range(2):
        arrived(0, l)
        arrived(0, 2 + l)
        parts = (w[0, 1 - l, 0], got[0, l], got[0, 2 + l])
        for k in range(3):
            both[k * FACE : (k + 1) * FACE, 0:128] = (w[0, l, k].astype(F32) + parts[k].astype(F32)).astype(BF16)
        for m in range(3):
            avg[l, m * FACE : (m + 1) * FACE, :] = mm(
                pt[l, m * FACE : (m + 1) * FACE, :], both[:, 0:128]
            ).astype(BF16)
        con[slot, l * PRIM : (l + 1) * PRIM, :] = mm(basis[l], avg[l]).astype(BF16)

    def send_con(j, _):
        mine_ = con.at[slot, pl.ds(0, BOTH)]
        pltpu.make_async_remote_copy(
            src_ref=mine_, dst_ref=mine_, send_sem=con_send, recv_sem=con_recv,
            device_id=near(j), device_id_type=MESH,
        ).start()
        return 0

    lax.fori_loop(1, 8, send_con, 0)

    loads[7].wait()
    for l in range(2):
        for m in range(3):
            loc[l, m * FACE : (m + 1) * FACE, :] = mm(linv[l, m * FACE : (m + 1) * FACE, :], avg[l])
    loads[8].wait()

    some = con.at[pl.ds(0, 7), pl.ds(0, BOTH)]
    pltpu.make_async_copy(some, some, con_recv).wait()
    every = con[...].reshape(8 * 128, RHS)
    for m in range(OWNERS // 4):
        rows = mm(oh1[m * 4 * PIECE : (m + 1) * 4 * PIECE, :], every).astype(BF16)
        rpart[m * 4 : (m + 1) * 4] = rows.reshape(4, PIECE, RHS)
    rs[mine] = rpart[mine]

    def spread(src, dst, send_sem, recv_sem, scattered):
        def send(j, _):
            to = ahead(j)
            if scattered:
                ts = to[1]
                owner = lax.rem(lax.div(ts, 4), 4) * 8 + lax.div(ts, 32) * 4 + lax.rem(ts, 4)
                piece = src.at[owner]
            else:
                piece = src.at[mine]
            pltpu.make_async_remote_copy(
                src_ref=piece, dst_ref=dst.at[mine], send_sem=send_sem, recv_sem=recv_sem,
                device_id=to, device_id_type=MESH,
            ).start()
            return 0

        lax.fori_loop(1, OWNERS, send, 0)

    def gathered(dst, recv_sem):
        pieces = dst.at[pl.ds(0, OWNERS - 1)]
        pltpu.make_async_copy(pieces, pieces, recv_sem).wait()

    spread(rpart, rs, rs_send, rs_recv, True)

    for q in range(4):
        c = pm_all[h * 4 + q].astype(F32)
        block = jnp.floor((c + 0.5) * (1.0 / 96.0))
        rem = c - 96.0 * block
        cx = jnp.floor((block + 0.5) * (1.0 / 32.0))
        cz = jnp.floor((block - 32.0 * cx + 0.5) * 0.25)
        cy = block - 32.0 * cx - 4.0 * cz
        ch = jnp.floor((cz + 0.5) * 0.25)
        ck = jnp.floor((rem + 0.5) * (1.0 / 48.0))
        owner = (cz - 4.0 * ch) * 8.0 + cx * 4.0 + cy
        code = (2.0 * ch + ck) * float(QUARTER) + owner * float(PIECE) + rem - 48.0 * ck
        code = jnp.where(c < 0.0, -1.0, code) - (p * QUARTER).astype(F32)
        col = column(code[0:1, :])
        for b in range(QUARTER // 128):
            lanes = lax.broadcasted_iota(I32, (128, 128), 1).astype(F32) + float(b * 128)
            oh2[q * 128 : (q + 1) * 128, b * 128 : (b + 1) * 128] = onehot(col == lanes)

    gathered(rs, rs_recv)

    def add_up(i, total):
        return total + rs[i].astype(F32)

    ag1[mine] = lax.fori_loop(1, OWNERS, add_up, rs[0].astype(F32)).astype(BF16)
    spread(ag1, ag1, ag1_send, ag1_recv, False)
    high = cinv[...].astype(BF16)
    low = (cinv[...] - high.astype(F32)).astype(BF16)
    gathered(ag1, ag1_recv)
    residual = ag1[...].reshape(QUARTER, RHS)
    part[...] = (mm(high, residual) + mm(low, residual)).reshape(2, PIECE, RHS)

    def part_copy(k, e):
        return pltpu.make_async_remote_copy(
            src_ref=part.at[k], dst_ref=pr.at[p], send_sem=pr_send.at[k, e], recv_sem=pr_recv,
            device_id=(2 * h + k, at(x, z + 4 * e, y)), device_id_type=MESH,
        )

    for k in range(2):
        part_copy(k, 1).start()

        @pl.when(p != 2 * h + k)
        def _():
            part_copy(k, 0).start()

        @pl.when(p == 2 * h + k)
        def _():
            pltpu.make_async_copy(part.at[k], pr.at[p], pr_recv).start()

    pltpu.make_async_copy(pr, pr, pr_recv).wait()
    ag2[mine] = (pr[0] + pr[1] + pr[2] + pr[3]).astype(BF16)
    spread(ag2, ag2, ag2_send, ag2_recv, False)
    gathered(ag2, ag2_recv)
    solved = ag2[...].reshape(QUARTER, RHS)
    for q in range(4):
        lp[q] = mm(oh2[q * 128 : q * 128 + BOTH, :], solved).astype(BF16)
    lr[p] = lp[p]

    def look_copy(j, _):
        to = lax.rem(p + j, 4)
        pltpu.make_async_remote_copy(
            src_ref=lp.at[to], dst_ref=lr.at[p], send_sem=lk_send, recv_sem=lk_recv,
            device_id=(to, s), device_id_type=MESH,
        ).start()
        return 0

    lax.fori_loop(1, 4, look_copy, 0)
    pltpu.make_async_copy(lr.at[pl.ds(0, 3)], lr.at[pl.ds(0, 3)], lk_recv).wait()
    total = lr[0].astype(F32) + lr[1].astype(F32) + lr[2].astype(F32) + lr[3].astype(F32)
    looked[0:BOTH, :] = total.astype(BF16)

    for l in range(2):
        for m in range(3):
            rows = slice(m * FACE, (m + 1) * FACE)
            vec[l, rows, :] = (loc[l, rows, :] + mm(bt[l, rows, :], looked[...])).astype(BF16)
    exchange(1, [vec[0], vec[1]], True)

    outs = []
    for l in range(2):
        arrived(1, l)
        arrived(1, 2 + l)
        parts = (w[1, 1 - l, 0], got[1, l], got[1, 2 + l])
        for k in range(3):
            both[k * FACE : (k + 1) * FACE, 0:128] = w[1, l, k]
            both[k * FACE : (k + 1) * FACE, 128:256] = parts[k]
        for m in range(3):
            pair = mm(pt[l, m * FACE : (m + 1) * FACE, :], both[...])
            outv[l, :, m * FACE : (m + 1) * FACE] = (pair[:, 0:128] + pair[:, 128:256]).T
        one = pltpu.make_async_copy(outv.at[l], out_h.at[l], out_sem.at[l])
        one.start()
        outs.append(one)

    for one in face_copies:
        one.wait_send()
    pltpu.make_async_copy(pm_all.at[pl.ds(0, 7)], pm_all.at[pl.ds(0, 7)], pm_send).wait()
    pltpu.make_async_copy(some, some, con_send).wait()
    gathered(rs, rs_send)
    gathered(ag1, ag1_send)
    gathered(ag2, ag2_send)
    pltpu.make_async_copy(lr.at[pl.ds(0, 3)], lr.at[pl.ds(0, 3)], lk_send).wait()
    for k in range(2):
        part_copy(k, 1).wait_send()

        @pl.when(p != 2 * h + k)
        def _():
            part_copy(k, 0).wait_send()

    for one in outs:
        one.wait()


def on_device(*operands):
    vmem, dma = pltpu.VMEM, pltpu.SemaphoreType.DMA
    return pl.pallas_call(
        kernel,
        out_shape=jax.ShapeDtypeStruct((2, RHS, IFACE), F32),
        in_specs=[pl.BlockSpec(memory_space=pl.ANY)] * 8,
        out_specs=pl.BlockSpec(memory_space=pl.ANY),
        scratch_shapes=[
            vmem((2, RHS, IFACE), BF16),
            vmem((2, IFACE, IFACE), BF16),
            vmem((2, 3, FACE, FACE), BF16),
            vmem((2, IFACE, IFACE), BF16),
            vmem((2, PRIM, IFACE), BF16),
            vmem((2, IFACE), I32),
            vmem((2, PRIM), I32),
            vmem((BOTH, QUARTER), F32),
            vmem((2, IFACE, IFACE), BF16),
            vmem((2, IFACE, IFACE), BF16),
            vmem((2, IFACE, RHS), BF16),
            vmem((2, IFACE, RHS), BF16),
            vmem((2, 2, 3, FACE, RHS), BF16),
            vmem((2, 4, FACE, RHS), BF16),
            vmem((IFACE, 2 * RHS), BF16),
            vmem((2, IFACE, RHS), BF16),
            vmem((2, IFACE, RHS), F32),
            vmem((2, 128, IFACE), F32),
            vmem((2, IFACE, 128), BF16),
            vmem((8, 128), I32),
            vmem((8, 8, 128), I32),
            vmem((8, 128, RHS), BF16),
            vmem((QUARTER, 1024), BF16),
            vmem((512, QUARTER), BF16),
            vmem((OWNERS, PIECE, RHS), BF16),
            vmem((OWNERS, PIECE, RHS), BF16),
            vmem((OWNERS, PIECE, RHS), BF16),
            vmem((2, PIECE, RHS), F32),
            vmem((4, PIECE, RHS), F32),
            vmem((OWNERS, PIECE, RHS), BF16),
            vmem((4, BOTH, RHS), BF16),
            vmem((4, BOTH, RHS), BF16),
            vmem((128, RHS), BF16),
            vmem((2, RHS, IFACE), F32),
            dma((9,)), dma((2,)), dma((2, 4)), dma((2, 4)), dma, dma, dma, dma,
            dma, dma, dma, dma, dma((2, 2)), dma, dma, dma, dma, dma,
        ],
        compiler_params=pltpu.CompilerParams(
            collective_id=0, has_side_effects=True, vmem_limit_bytes=48 * 1024 * 1024
        ),
        cost_estimate=pl.CostEstimate(flops=3_000_000_000, bytes_accessed=9_000_000, transcendentals=0),
    )(*operands)


def solution(mesh):
    return jax.shard_map(
        on_device,
        mesh=mesh,
        in_specs=(
            P(("plane", "sub"), None, None),
            P(("plane", "sub"), None, None),
            P(("plane", "sub"), None, None, None),
            P(("plane", "sub"), None, None),
            P(("plane", "sub"), None, None),
            P(("plane", "sub"), None),
            P(("plane", "sub"), None),
            P("sub", None),
        ),
        out_specs=P(("plane", "sub"), None, None),
        check_vma=False,
    )
```

```python
import jax
import jax.numpy as jnp
from jax import lax
from jax.experimental import pallas as pl
from jax.experimental.pallas import tpu as pltpu
from jax.sharding import PartitionSpec as P

MESH = pl.DeviceIdType.MESH
F32, BF16, I32 = jnp.float32, jnp.bfloat16, jnp.int32
RHS, IFACE, FACE, PRIM = 128, 768, 256, 48
BOTH = 2 * PRIM
QUARTER = 1536
OWNERS = 32
PIECE = QUARTER // OWNERS


def mm(a, b):
    return jnp.dot(a, b, preferred_element_type=F32)


def onehot(mask):
    return jnp.where(mask, 1.0, 0.0).astype(BF16)


def column(row):
    return jnp.broadcast_to(row, (128, 128)).T


def kernel(
    res_h, schur_h, finv_h, linv_h, basis_h, fd_h, pm_h, cinv_h, out_h,
    res, schur, finv, linv, basis, fd, pm, cinv,
    pt, pp, img, vec, w, got, both, avg, loc, bpad, bt,
    pm_row, pm_all, con, oh1, oh2, rpart, rs, zs, zr, ag1, part, pr, ag2, lp, lr, looked, outv,
    load_sem, out_sem, face_send, face_recv, pm_send, pm_recv, con_send, con_recv,
    rs_send, rs_recv, zr_send, zr_recv, ag1_send, ag1_z, ag1_recv, pr_send, pr_recv,
    ag2_send, ag2_z, ag2_recv, lk_send, lk_recv,
):
    p, s = lax.axis_index("plane"), lax.axis_index("sub")
    x, z, y = lax.div(s, 32), lax.rem(lax.div(s, 4), 8), lax.rem(s, 4)
    pair, odd = lax.div(z, 2), lax.rem(z, 2)
    sign = 2 * odd - 1
    xy = x * 4 + y
    mine = xy * 4 + pair

    def at(ax, az, ay):
        return lax.rem(ax, 2) * 32 + lax.rem(az, 8) * 4 + lax.rem(ay, 4)

    def along(j):
        return p, at(x, z + 8 + sign * j, y)

    def source(j):
        return lax.rem(z + 8 + (sign * j if j % 2 else -sign * j), 8)

    def across(i):
        return p, at(x + lax.div(i, 4), z, y + lax.rem(i, 4))

    def near(j):
        return lax.rem(p + lax.rem(j, 4), 4), at(x, z + 8 - sign * lax.div(j, 4), y)

    up, down = lax.rem(s + 1, 64), lax.rem(s + 63, 64)
    core = p + 1 - 2 * lax.rem(p, 2)
    far = p + 2 - 4 * lax.div(p, 2)

    def load(i, src, dst):
        return pltpu.make_async_copy(src, dst, load_sem.at[i])

    loads = [
        load(0, fd_h, fd),
        load(1, pm_h, pm),
        load(2, res_h, res),
        load(3, schur_h.at[0], schur.at[0]),
        load(4, schur_h.at[1], schur.at[1]),
        load(5, finv_h, finv),
        load(6, basis_h, basis),
        load(7, linv_h, linv),
        load(8, cinv_h.at[:, pl.ds(pl.multiple_of(p * QUARTER, QUARTER), QUARTER)], cinv),
    ]
    for one in loads:
        one.start()

    con[...] = jnp.zeros_like(con)
    looked[...] = jnp.zeros_like(looked)
    barrier = pltpu.get_barrier_semaphore()

    def greet(to):
        pl.semaphore_signal(barrier, inc=1, device_id=to, device_id_type=MESH)

    def greet_across(i, _):
        greet(across(i))
        return 0

    def greet_near(j, _):
        greet(near(j))
        return 0

    for j in (1, 2, 3):
        greet((p, at(x, source(j), y)))
    lax.fori_loop(1, 8, greet_across, 0)
    lax.fori_loop(1, 8, greet_near, 0)
    greet((p, up))
    greet((p, down))

    loads[0].wait()
    for l in range(2):
        row = fd[l : l + 1, :].astype(F32)
        for m in range(3):
            rows = lax.broadcasted_iota(I32, (FACE, IFACE), 0).astype(F32) + float(m * FACE)
            pt[l, m * FACE : (m + 1) * FACE, :] = onehot(rows == row)
        for b in range(6):
            col = column(row[:, b * 128 : (b + 1) * 128])
            for c in range(6):
                lanes = lax.broadcasted_iota(I32, (128, 128), 1).astype(F32) + float(c * 128)
                pp[l, b * 128 : (b + 1) * 128, c * 128 : (c + 1) * 128] = onehot(col == lanes)

    loads[1].wait()
    pm_row[...] = jnp.full((8, 128), -1, I32)
    pm_row[0:2, 0:PRIM] = pm[...]
    first = pm_row[0:1, :]
    second = pltpu.roll(jnp.broadcast_to(pm_row[1:2, :], (8, 128)), PRIM, 1)
    lane = lax.broadcasted_iota(I32, (8, 128), 1)
    pm_row[...] = jnp.where(lane < PRIM, jnp.broadcast_to(first, (8, 128)), jnp.where(lane < BOTH, second, -1))
    slot = odd * 4 + p
    pm_all[slot] = pm_row[...]

    def image(l, vector, transposed):
        for m in range(3):
            rows = schur[l, m * FACE : (m + 1) * FACE, :]
            if transposed:
                part_ = mm(rows, vector)
            else:
                part_ = lax.dot_general(rows, vector, (((1,), (1,)), ((), ())), preferred_element_type=F32)
            img[l, m * FACE : (m + 1) * FACE, :] = part_.astype(BF16)

    def weigh(d, l, k):
        faces = mm(pp[l, k * FACE : (k + 1) * FACE, :], img[l]).astype(BF16)
        w[d, l, k] = mm(finv[l, k], faces).astype(BF16)

    def face_copy(d, l, k):
        if k == 1:
            to, there = (p, down if l == 0 else up), 1 - l
        else:
            to, there = (core if l == 0 else far, s), 2 + l
        here = 2 * (k - 1) + l
        return pltpu.make_async_remote_copy(
            src_ref=w.at[d, l, k],
            dst_ref=got.at[d, there],
            send_sem=face_send.at[d, here],
            recv_sem=face_recv.at[d, there],
            device_id=to,
            device_id_type=MESH,
        )

    def arrived(d, slot_):
        pltpu.make_async_copy(got.at[d, slot_], got.at[d, slot_], face_recv.at[d, slot_]).wait()

    face_copies = []

    def exchange(d, vectors, transposed):
        for l in range(2):
            image(l, vectors[l], transposed)
            for k in (1, 2):
                weigh(d, l, k)
                if d == 0 and l == 0 and k == 1:
                    pl.semaphore_wait(barrier, 3 + 7 + 7 + 2)
                    lax.fori_loop(1, 8, send_pm, 0)
                one = face_copy(d, l, k)
                one.start()
                face_copies.append(one)
        for l in range(2):
            weigh(d, l, 0)

    def send_pm(j, _):
        pltpu.make_async_remote_copy(
            src_ref=pm_row, dst_ref=pm_all.at[slot], send_sem=pm_send, recv_sem=pm_recv,
            device_id=near(j), device_id_type=MESH,
        ).start()
        return 0

    loads[2].wait()
    loads[3].wait()
    loads[4].wait()
    loads[5].wait()
    exchange(0, [res[0], res[1]], False)

    loads[6].wait()
    bpad[...] = jnp.zeros_like(bpad)
    for l in range(2):
        bpad[l, l * PRIM : (l + 1) * PRIM, :] = basis[l].astype(F32)
        for b in range(6):
            bt[l, b * 128 : (b + 1) * 128, :] = bpad[l, :, b * 128 : (b + 1) * 128].T.astype(BF16)
    pltpu.make_async_copy(pm_all.at[pl.ds(0, 7)], pm_all.at[pl.ds(0, 7)], pm_recv).wait()
    for t in range(8):
        row = pm_all[t, 0:1, :].astype(F32) - (p * QUARTER).astype(F32)
        for m in range(6):
            rows = lax.broadcasted_iota(I32, (256, 128), 0).astype(F32) + float(m * 256)
            oh1[m * 256 : (m + 1) * 256, t * 128 : (t + 1) * 128] = onehot(rows == row)

    for l in range(2):
        arrived(0, l)
        arrived(0, 2 + l)
        parts = (w[0, 1 - l, 0], got[0, l], got[0, 2 + l])
        for k in range(3):
            both[k * FACE : (k + 1) * FACE, 0:128] = (w[0, l, k].astype(F32) + parts[k].astype(F32)).astype(BF16)
        for m in range(3):
            avg[l, m * FACE : (m + 1) * FACE, :] = mm(
                pt[l, m * FACE : (m + 1) * FACE, :], both[:, 0:128]
            ).astype(BF16)
        con[slot, l * PRIM : (l + 1) * PRIM, :] = mm(basis[l], avg[l]).astype(BF16)

    def send_con(j, _):
        mine_ = con.at[slot, pl.ds(0, BOTH)]
        pltpu.make_async_remote_copy(
            src_ref=mine_, dst_ref=mine_, send_sem=con_send, recv_sem=con_recv,
            device_id=near(j), device_id_type=MESH,
        ).start()
        return 0

    lax.fori_loop(1, 8, send_con, 0)

    loads[7].wait()
    for l in range(2):
        for m in range(3):
            loc[l, m * FACE : (m + 1) * FACE, :] = mm(linv[l, m * FACE : (m + 1) * FACE, :], avg[l])
    loads[8].wait()

    some = con.at[pl.ds(0, 7), pl.ds(0, BOTH)]
    pltpu.make_async_copy(some, some, con_recv).wait()
    every = con[...].reshape(8 * 128, RHS)
    for m in range(OWNERS // 4):
        rows = mm(oh1[m * 4 * PIECE : (m + 1) * 4 * PIECE, :], every).astype(BF16)
        rpart[m * 4 : (m + 1) * 4] = rows.reshape(4, PIECE, RHS)

    far_pair = lax.rem(pair + 2, 4)
    next_pair = lax.rem(pair + 4 + sign, 4)
    for n, target in enumerate((far_pair, next_pair, pair)):

        def send_rs(i, _, n=n, target=target):
            to = across(i)
            txy = lax.div(to[1], 32) * 4 + lax.rem(to[1], 4)
            pltpu.make_async_remote_copy(
                src_ref=rpart.at[txy * 4 + target], dst_ref=rs.at[n, xy], send_sem=rs_send, recv_sem=rs_recv.at[n],
                device_id=to, device_id_type=MESH,
            ).start()
            return 0

        lax.fori_loop(1, 8, send_rs, 0)
        rs[n, xy] = rpart[xy * 4 + target]

    for q in range(4):
        c = pm_all[odd * 4 + q].astype(F32)
        block = jnp.floor((c + 0.5) * (1.0 / 96.0))
        rem = c - 96.0 * block
        cx = jnp.floor((block + 0.5) * (1.0 / 32.0))
        cz = jnp.floor((block - 32.0 * cx + 0.5) * 0.25)
        cy = block - 32.0 * cx - 4.0 * cz
        cg = jnp.floor((cz + 0.5) * 0.5)
        ck = jnp.floor((rem + 0.5) * (1.0 / 48.0))
        owner = (cx * 4.0 + cy) * 4.0 + cg
        code = (2.0 * (cz - 2.0 * cg) + ck) * float(QUARTER) + owner * float(PIECE) + rem - 48.0 * ck
        code = jnp.where(c < 0.0, -1.0, code) - (p * QUARTER).astype(F32)
        col = column(code[0:1, :])
        for b in range(QUARTER // 128):
            lanes = lax.broadcasted_iota(I32, (128, 128), 1).astype(F32) + float(b * 128)
            oh2[q * 128 : (q + 1) * 128, b * 128 : (b + 1) * 128] = onehot(col == lanes)

    def z_copy(src, j, n):
        return pltpu.make_async_remote_copy(
            src_ref=src, dst_ref=zr.at[j - 1], send_sem=zr_send, recv_sem=zr_recv.at[j - 1],
            device_id=along(j), device_id_type=MESH,
        )

    for n in range(3):
        seven = rs.at[n, pl.ds(0, 7)]
        pltpu.make_async_copy(seven, seven, rs_recv.at[n]).wait()
        total = rs[n, 0].astype(F32)
        for i in range(1, 8):
            total = total + rs[n, i].astype(F32)
        if n < 2:
            zs[n] = total.astype(BF16)
            for j in ((3,), (2, 1))[n]:
                z_copy(zs.at[n], j, n).start()
    for j in (1, 2, 3):
        pltpu.make_async_copy(zr.at[j - 1], zr.at[j - 1], zr_recv.at[j - 1]).wait()
        total = total + zr[j - 1].astype(F32)

    def gather_start(buf, sems):
        send_sem, z_recv, xy_recv = sems
        own = buf.at[mine]
        for j in (3, 2, 1):
            pltpu.make_async_remote_copy(
                src_ref=own, dst_ref=own, send_sem=send_sem, recv_sem=z_recv.at[j - 1],
                device_id=along(j), device_id_type=MESH,
            ).start()
        relay(buf, mine, sems)

    def relay(buf, owner, sems):
        send_sem, _, xy_recv = sems
        piece = buf.at[owner]

        def send(i, _):
            pltpu.make_async_remote_copy(
                src_ref=piece, dst_ref=piece, send_sem=send_sem, recv_sem=xy_recv,
                device_id=across(i), device_id_type=MESH,
            ).start()
            return 0

        lax.fori_loop(1, 8, send, 0)

    def gather_finish(buf, sems):
        _, z_recv, xy_recv = sems
        for j in (1, 2, 3):
            owner = xy * 4 + lax.div(source(j), 2)
            pltpu.make_async_copy(buf.at[owner], buf.at[owner], z_recv.at[j - 1]).wait()
            relay(buf, owner, sems)
        pieces = buf.at[pl.ds(0, 28)]
        pltpu.make_async_copy(pieces, pieces, xy_recv).wait()

    ag1[mine] = total.astype(BF16)
    sems1 = (ag1_send, ag1_z, ag1_recv)
    gather_start(ag1, sems1)
    high = cinv[...].astype(BF16)
    low = (cinv[...] - high.astype(F32)).astype(BF16)
    gather_finish(ag1, sems1)
    residual = ag1[...].reshape(QUARTER, RHS)
    part[...] = (mm(high, residual) + mm(low, residual)).reshape(2, PIECE, RHS)

    def part_copy(k, e):
        return pltpu.make_async_remote_copy(
            src_ref=part.at[k], dst_ref=pr.at[p], send_sem=pr_send.at[k, e], recv_sem=pr_recv,
            device_id=(2 * odd + k, at(x, z + 8 - sign * e, y)), device_id_type=MESH,
        )

    for k in range(2):
        part_copy(k, 1).start()

        @pl.when(p != 2 * odd + k)
        def _():
            part_copy(k, 0).start()

        @pl.when(p == 2 * odd + k)
        def _():
            pltpu.make_async_copy(part.at[k], pr.at[p], pr_recv).start()

    pltpu.make_async_copy(pr, pr, pr_recv).wait()
    ag2[mine] = (pr[0] + pr[1] + pr[2] + pr[3]).astype(BF16)
    sems2 = (ag2_send, ag2_z, ag2_recv)
    gather_start(ag2, sems2)
    gather_finish(ag2, sems2)
    solved = ag2[...].reshape(QUARTER, RHS)
    for q in range(4):
        lp[q] = mm(oh2[q * 128 : q * 128 + BOTH, :], solved).astype(BF16)
    lr[p] = lp[p]

    def look_copy(j, _):
        to = lax.rem(p + j, 4)
        pltpu.make_async_remote_copy(
            src_ref=lp.at[to], dst_ref=lr.at[p], send_sem=lk_send, recv_sem=lk_recv,
            device_id=(to, s), device_id_type=MESH,
        ).start()
        return 0

    lax.fori_loop(1, 4, look_copy, 0)
    pltpu.make_async_copy(lr.at[pl.ds(0, 3)], lr.at[pl.ds(0, 3)], lk_recv).wait()
    total = lr[0].astype(F32) + lr[1].astype(F32) + lr[2].astype(F32) + lr[3].astype(F32)
    looked[0:BOTH, :] = total.astype(BF16)

    for l in range(2):
        for m in range(3):
            rows = slice(m * FACE, (m + 1) * FACE)
            vec[l, rows, :] = (loc[l, rows, :] + mm(bt[l, rows, :], looked[...])).astype(BF16)
    exchange(1, [vec[0], vec[1]], True)

    outs = []
    for l in range(2):
        arrived(1, l)
        arrived(1, 2 + l)
        parts = (w[1, 1 - l, 0], got[1, l], got[1, 2 + l])
        for k in range(3):
            both[k * FACE : (k + 1) * FACE, 0:128] = w[1, l, k]
            both[k * FACE : (k + 1) * FACE, 128:256] = parts[k]
        for m in range(3):
            pair = mm(pt[l, m * FACE : (m + 1) * FACE, :], both[...])
            outv[l, :, m * FACE : (m + 1) * FACE] = (pair[:, 0:128] + pair[:, 128:256]).T
        one = pltpu.make_async_copy(outv.at[l], out_h.at[l], out_sem.at[l])
        one.start()
        outs.append(one)

    for one in face_copies:
        one.wait_send()
    pltpu.make_async_copy(pm_all.at[pl.ds(0, 7)], pm_all.at[pl.ds(0, 7)], pm_send).wait()
    pltpu.make_async_copy(some, some, con_send).wait()
    for buf, sem, count in ((rpart, rs_send, 21), (zr, zr_send, 3), (ag1, ag1_send, 31), (ag2, ag2_send, 31)):
        sent = buf.at[pl.ds(0, count)]
        pltpu.make_async_copy(sent, sent, sem).wait()
    pltpu.make_async_copy(lr.at[pl.ds(0, 3)], lr.at[pl.ds(0, 3)], lk_send).wait()
    for k in range(2):
        part_copy(k, 1).wait_send()

        @pl.when(p != 2 * odd + k)
        def _():
            part_copy(k, 0).wait_send()

    for one in outs:
        one.wait()


def on_device(*operands):
    vmem, dma = pltpu.VMEM, pltpu.SemaphoreType.DMA
    return pl.pallas_call(
        kernel,
        out_shape=jax.ShapeDtypeStruct((2, RHS, IFACE), F32),
        in_specs=[pl.BlockSpec(memory_space=pl.ANY)] * 8,
        out_specs=pl.BlockSpec(memory_space=pl.ANY),
        scratch_shapes=[
            vmem((2, RHS, IFACE), BF16),
            vmem((2, IFACE, IFACE), BF16),
            vmem((2, 3, FACE, FACE), BF16),
            vmem((2, IFACE, IFACE), BF16),
            vmem((2, PRIM, IFACE), BF16),
            vmem((2, IFACE), I32),
            vmem((2, PRIM), I32),
            vmem((BOTH, QUARTER), F32),
            vmem((2, IFACE, IFACE), BF16),
            vmem((2, IFACE, IFACE), BF16),
            vmem((2, IFACE, RHS), BF16),
            vmem((2, IFACE, RHS), BF16),
            vmem((2, 2, 3, FACE, RHS), BF16),
            vmem((2, 4, FACE, RHS), BF16),
            vmem((IFACE, 2 * RHS), BF16),
            vmem((2, IFACE, RHS), BF16),
            vmem((2, IFACE, RHS), F32),
            vmem((2, 128, IFACE), F32),
            vmem((2, IFACE, 128), BF16),
            vmem((8, 128), I32),
            vmem((8, 8, 128), I32),
            vmem((8, 128, RHS), BF16),
            vmem((QUARTER, 1024), BF16),
            vmem((512, QUARTER), BF16),
            vmem((OWNERS, PIECE, RHS), BF16),
            vmem((3, 8, PIECE, RHS), BF16),
            vmem((2, PIECE, RHS), BF16),
            vmem((3, PIECE, RHS), BF16),
            vmem((OWNERS, PIECE, RHS), BF16),
            vmem((2, PIECE, RHS), F32),
            vmem((4, PIECE, RHS), F32),
            vmem((OWNERS, PIECE, RHS), BF16),
            vmem((4, BOTH, RHS), BF16),
            vmem((4, BOTH, RHS), BF16),
            vmem((128, RHS), BF16),
            vmem((2, RHS, IFACE), F32),
            dma((9,)), dma((2,)), dma((2, 4)), dma((2, 4)), dma, dma, dma, dma,
            dma, dma((3,)), dma, dma((3,)), dma, dma((3,)), dma, dma((2, 2)), dma, dma, dma((3,)), dma, dma, dma,
        ],
        compiler_params=pltpu.CompilerParams(
            collective_id=0, has_side_effects=True, vmem_limit_bytes=62 * 1024 * 1024
        ),
        cost_estimate=pl.CostEstimate(flops=3_000_000_000, bytes_accessed=9_000_000, transcendentals=0),
    )(*operands)


def solution(mesh):
    return jax.shard_map(
        on_device,
        mesh=mesh,
        in_specs=(
            P(("plane", "sub"), None, None),
            P(("plane", "sub"), None, None),
            P(("plane", "sub"), None, None, None),
            P(("plane", "sub"), None, None),
            P(("plane", "sub"), None, None),
            P(("plane", "sub"), None),
            P(("plane", "sub"), None),
            P("sub", None),
        ),
        out_specs=P(("plane", "sub"), None, None),
        check_vma=False,
    )
```

```python
import jax
import jax.numpy as jnp
from jax import lax
from jax.experimental import pallas as pl
from jax.experimental.pallas import tpu as pltpu
from jax.sharding import PartitionSpec as P

MESH = pl.DeviceIdType.MESH
F32, BF16, I32 = jnp.float32, jnp.bfloat16, jnp.int32
RHS, IFACE, FACE, PRIM = 128, 768, 256, 48
BOTH = 2 * PRIM
QUARTER = 1536
OWNERS = 32
PIECE = QUARTER // OWNERS


def mm(a, b):
    return jnp.dot(a, b, preferred_element_type=F32)


def onehot(mask):
    return jnp.where(mask, 1.0, 0.0).astype(BF16)


def column(row):
    return jnp.broadcast_to(row, (128, 128)).T


def kernel(
    res_h, schur_h, finv_h, linv_h, basis_h, fd_h, pm_h, cinv_h, out_h,
    res, schur, finv, linv, basis, fd, pm, cinv,
    pt, pp, sp, img, vec, w, got, acc, avg, loc, bpad, bt,
    pm_row, pm_all, con, oh1, oh2, rpart, rs, zs, zr, ag1, part, pr, ag2, lp, lr, looked, outv,
    load_sem, out_sem, face_send, face_recv, pm_send, pm_recv, con_send, con_recv,
    rs_send, rs_recv, zr_send, zr_recv, ag1_send, ag1_z, ag1_recv, pr_send, pr_recv,
    ag2_send, ag2_z, ag2_recv, lk_send, lk_recv,
):
    p, s = lax.axis_index("plane"), lax.axis_index("sub")
    x, z, y = lax.div(s, 32), lax.rem(lax.div(s, 4), 8), lax.rem(s, 4)
    pair, odd = lax.div(z, 2), lax.rem(z, 2)
    sign = 2 * odd - 1
    xy = x * 4 + y
    mine = xy * 4 + pair

    def at(ax, az, ay):
        return lax.rem(ax, 2) * 32 + lax.rem(az, 8) * 4 + lax.rem(ay, 4)

    def along(j):
        return p, at(x, z + 8 + sign * j, y)

    def source(j):
        return lax.rem(z + 8 + (sign * j if j % 2 else -sign * j), 8)

    def across(i):
        return p, at(x + lax.div(i, 4), z, y + lax.rem(i, 4))

    def near(j):
        return lax.rem(p + lax.rem(j, 4), 4), at(x, z + 8 - sign * lax.div(j, 4), y)

    up, down = lax.rem(s + 1, 64), lax.rem(s + 63, 64)
    core = p + 1 - 2 * lax.rem(p, 2)
    far = p + 2 - 4 * lax.div(p, 2)

    def load(i, src, dst):
        return pltpu.make_async_copy(src, dst, load_sem.at[i])

    loads = [
        load(0, fd_h, fd),
        load(1, pm_h, pm),
        load(2, res_h, res),
        load(3, schur_h.at[0], schur.at[0]),
        load(4, schur_h.at[1], schur.at[1]),
        load(5, finv_h, finv),
        load(6, basis_h, basis),
        load(7, linv_h, linv),
        load(8, cinv_h.at[:, pl.ds(pl.multiple_of(p * QUARTER, QUARTER), QUARTER)], cinv),
    ]
    for one in loads:
        one.start()

    con[...] = jnp.zeros_like(con)
    looked[...] = jnp.zeros_like(looked)
    barrier = pltpu.get_barrier_semaphore()

    def greet(to):
        pl.semaphore_signal(barrier, inc=1, device_id=to, device_id_type=MESH)

    def greet_across(i, _):
        greet(across(i))
        return 0

    def greet_near(j, _):
        greet(near(j))
        return 0

    for j in (1, 2, 3):
        greet((p, at(x, source(j), y)))
    lax.fori_loop(1, 8, greet_across, 0)
    lax.fori_loop(1, 8, greet_near, 0)
    greet((p, up))
    greet((p, down))

    loads[0].wait()
    for l in range(2):
        row = fd[l : l + 1, :].astype(F32)
        for b in range(6):
            col = column(row[:, b * 128 : (b + 1) * 128])
            for c in range(6):
                lanes = lax.broadcasted_iota(I32, (128, 128), 1).astype(F32) + float(c * 128)
                pp[l, b * 128 : (b + 1) * 128, c * 128 : (c + 1) * 128] = onehot(col == lanes)

    loads[1].wait()
    pm_row[...] = jnp.full((8, 128), -1, I32)
    pm_row[0:2, 0:PRIM] = pm[...]
    first = pm_row[0:1, :]
    second = pltpu.roll(jnp.broadcast_to(pm_row[1:2, :], (8, 128)), PRIM, 1)
    lane = lax.broadcasted_iota(I32, (8, 128), 1)
    pm_row[...] = jnp.where(lane < PRIM, jnp.broadcast_to(first, (8, 128)), jnp.where(lane < BOTH, second, -1))
    slot = odd * 4 + p
    pm_all[slot] = pm_row[...]

    def image(l):
        for m in range(3):
            rows = slice(m * FACE, (m + 1) * FACE)
            img[l, rows, :] = lax.dot_general(
                schur[l, rows, :], res[l], (((1,), (1,)), ((), ())), preferred_element_type=F32
            ).astype(BF16)

    def weigh(d, l, k):
        rows = slice(k * FACE, (k + 1) * FACE)
        if d == 0:
            faces = mm(pp[l, rows, :], img[l])
        else:
            faces = mm(sp[l, rows, :], vec[l])
        w[d, l, k] = mm(finv[l, k], faces.astype(BF16)).astype(BF16)

    def prepare(l):
        for k in range(3):
            rows = slice(k * FACE, (k + 1) * FACE)
            sp[l, rows, :] = mm(pp[l, rows, :], schur[l]).astype(BF16)

    def face_copy(d, l, k):
        if k == 1:
            to, there = (p, down if l == 0 else up), 1 - l
        else:
            to, there = (core if l == 0 else far, s), l
        return pltpu.make_async_remote_copy(
            src_ref=w.at[d, l, k],
            dst_ref=got.at[d, there, k - 1],
            send_sem=face_send.at[d, l, k - 1],
            recv_sem=face_recv.at[d, there, k - 1],
            device_id=to,
            device_id_type=MESH,
        )

    def arrived(d, l):
        for k in range(2):
            pltpu.make_async_copy(got.at[d, l, k], got.at[d, l, k], face_recv.at[d, l, k]).wait()

    def permute_own(d):
        for l in range(2):
            for m in range(3):
                rows = slice(m * FACE, (m + 1) * FACE)
                acc[l, rows, :] = mm(pt[l, rows, :], w[d, l].reshape(IFACE, RHS)) + mm(
                    pt[l, rows, 0:FACE], w[d, 1 - l, 0]
                )

    def permuted(d, l, m):
        rows = slice(m * FACE, (m + 1) * FACE)
        return acc[l, rows, :] + mm(pt[l, rows, FACE:], got[d, l].reshape(2 * FACE, RHS))

    face_copies = []

    def exchange(d):
        for l in range(2):
            if d == 0:
                image(l)
            for k in (1, 2):
                weigh(d, l, k)
                if d == 0 and l == 0 and k == 1:
                    pl.semaphore_wait(barrier, 3 + 7 + 7 + 2)
                    lax.fori_loop(1, 8, send_pm, 0)
                one = face_copy(d, l, k)
                one.start()
                face_copies.append(one)
        for l in range(2):
            weigh(d, l, 0)

    def send_pm(j, _):
        pltpu.make_async_remote_copy(
            src_ref=pm_row, dst_ref=pm_all.at[slot], send_sem=pm_send, recv_sem=pm_recv,
            device_id=near(j), device_id_type=MESH,
        ).start()
        return 0

    loads[2].wait()
    loads[3].wait()
    loads[4].wait()
    loads[5].wait()
    exchange(0)

    for l in range(2):
        row = fd[l : l + 1, :].astype(F32)
        for m in range(3):
            rows = lax.broadcasted_iota(I32, (FACE, IFACE), 0).astype(F32) + float(m * FACE)
            pt[l, m * FACE : (m + 1) * FACE, :] = onehot(rows == row)
    permute_own(0)
    loads[6].wait()
    bpad[...] = jnp.zeros_like(bpad)
    for l in range(2):
        bpad[l, l * PRIM : (l + 1) * PRIM, :] = basis[l].astype(F32)
        for b in range(6):
            bt[l, b * 128 : (b + 1) * 128, :] = bpad[l, :, b * 128 : (b + 1) * 128].T.astype(BF16)
    pltpu.make_async_copy(pm_all.at[pl.ds(0, 7)], pm_all.at[pl.ds(0, 7)], pm_recv).wait()
    for t in range(8):
        row = pm_all[t, 0:1, :].astype(F32) - (p * QUARTER).astype(F32)
        for m in range(6):
            rows = lax.broadcasted_iota(I32, (256, 128), 0).astype(F32) + float(m * 256)
            oh1[m * 256 : (m + 1) * 256, t * 128 : (t + 1) * 128] = onehot(rows == row)

    for l in range(2):
        arrived(0, l)
        for m in range(3):
            avg[l, m * FACE : (m + 1) * FACE, :] = permuted(0, l, m).astype(BF16)
        con[slot, l * PRIM : (l + 1) * PRIM, :] = mm(basis[l], avg[l]).astype(BF16)

    def send_con(j, _):
        mine_ = con.at[slot, pl.ds(0, BOTH)]
        pltpu.make_async_remote_copy(
            src_ref=mine_, dst_ref=mine_, send_sem=con_send, recv_sem=con_recv,
            device_id=near(j), device_id_type=MESH,
        ).start()
        return 0

    lax.fori_loop(1, 8, send_con, 0)

    loads[7].wait()
    for l in range(2):
        for m in range(3):
            loc[l, m * FACE : (m + 1) * FACE, :] = mm(linv[l, m * FACE : (m + 1) * FACE, :], avg[l])
    loads[8].wait()

    some = con.at[pl.ds(0, 7), pl.ds(0, BOTH)]
    pltpu.make_async_copy(some, some, con_recv).wait()
    every = con[...].reshape(8 * 128, RHS)
    for m in range(OWNERS // 4):
        rows = mm(oh1[m * 4 * PIECE : (m + 1) * 4 * PIECE, :], every).astype(BF16)
        rpart[m * 4 : (m + 1) * 4] = rows.reshape(4, PIECE, RHS)

    far_pair = lax.rem(pair + 2, 4)
    next_pair = lax.rem(pair + 4 + sign, 4)
    for n, target in enumerate((far_pair, next_pair, pair)):

        def send_rs(i, _, n=n, target=target):
            to = across(i)
            txy = lax.div(to[1], 32) * 4 + lax.rem(to[1], 4)
            pltpu.make_async_remote_copy(
                src_ref=rpart.at[txy * 4 + target], dst_ref=rs.at[n, xy], send_sem=rs_send, recv_sem=rs_recv.at[n],
                device_id=to, device_id_type=MESH,
            ).start()
            return 0

        lax.fori_loop(1, 8, send_rs, 0)
        rs[n, xy] = rpart[xy * 4 + target]

    for q in range(4):
        c = pm_all[odd * 4 + q].astype(F32)
        block = jnp.floor((c + 0.5) * (1.0 / 96.0))
        rem = c - 96.0 * block
        cx = jnp.floor((block + 0.5) * (1.0 / 32.0))
        cz = jnp.floor((block - 32.0 * cx + 0.5) * 0.25)
        cy = block - 32.0 * cx - 4.0 * cz
        cg = jnp.floor((cz + 0.5) * 0.5)
        ck = jnp.floor((rem + 0.5) * (1.0 / 48.0))
        owner = (cx * 4.0 + cy) * 4.0 + cg
        code = (2.0 * (cz - 2.0 * cg) + ck) * float(QUARTER) + owner * float(PIECE) + rem - 48.0 * ck
        code = jnp.where(c < 0.0, -1.0, code) - (p * QUARTER).astype(F32)
        col = column(code[0:1, :])
        for b in range(QUARTER // 128):
            lanes = lax.broadcasted_iota(I32, (128, 128), 1).astype(F32) + float(b * 128)
            oh2[q * 128 : (q + 1) * 128, b * 128 : (b + 1) * 128] = onehot(col == lanes)

    prepare(0)

    def z_copy(src, j, n):
        return pltpu.make_async_remote_copy(
            src_ref=src, dst_ref=zr.at[j - 1], send_sem=zr_send, recv_sem=zr_recv.at[j - 1],
            device_id=along(j), device_id_type=MESH,
        )

    for n in range(3):
        seven = rs.at[n, pl.ds(0, 7)]
        pltpu.make_async_copy(seven, seven, rs_recv.at[n]).wait()
        total = rs[n, 0].astype(F32)
        for i in range(1, 8):
            total = total + rs[n, i].astype(F32)
        if n < 2:
            zs[n] = total.astype(BF16)
            for j in ((3,), (2, 1))[n]:
                z_copy(zs.at[n], j, n).start()
    for j in (1, 2, 3):
        pltpu.make_async_copy(zr.at[j - 1], zr.at[j - 1], zr_recv.at[j - 1]).wait()
        total = total + zr[j - 1].astype(F32)

    def gather_start(buf, sems):
        send_sem, z_recv, xy_recv = sems
        own = buf.at[mine]
        for j in (3, 2, 1):
            pltpu.make_async_remote_copy(
                src_ref=own, dst_ref=own, send_sem=send_sem, recv_sem=z_recv.at[j - 1],
                device_id=along(j), device_id_type=MESH,
            ).start()
        relay(buf, mine, sems)

    def relay(buf, owner, sems):
        send_sem, _, xy_recv = sems
        piece = buf.at[owner]

        def send(i, _):
            pltpu.make_async_remote_copy(
                src_ref=piece, dst_ref=piece, send_sem=send_sem, recv_sem=xy_recv,
                device_id=across(i), device_id_type=MESH,
            ).start()
            return 0

        lax.fori_loop(1, 8, send, 0)

    def gather_finish(buf, sems):
        _, z_recv, xy_recv = sems
        for j in (1, 2, 3):
            owner = xy * 4 + lax.div(source(j), 2)
            pltpu.make_async_copy(buf.at[owner], buf.at[owner], z_recv.at[j - 1]).wait()
            relay(buf, owner, sems)
        pieces = buf.at[pl.ds(0, 28)]
        pltpu.make_async_copy(pieces, pieces, xy_recv).wait()

    ag1[mine] = total.astype(BF16)
    sems1 = (ag1_send, ag1_z, ag1_recv)
    gather_start(ag1, sems1)
    prepare(1)
    high = cinv[...].astype(BF16)
    low = (cinv[...] - high.astype(F32)).astype(BF16)
    gather_finish(ag1, sems1)
    residual = ag1[...].reshape(QUARTER, RHS)
    part[...] = (mm(high, residual) + mm(low, residual)).astype(BF16).reshape(2, PIECE, RHS)

    def part_copy(k, e):
        return pltpu.make_async_remote_copy(
            src_ref=part.at[k], dst_ref=pr.at[p], send_sem=pr_send.at[k, e], recv_sem=pr_recv,
            device_id=(2 * odd + k, at(x, z + 8 - sign * e, y)), device_id_type=MESH,
        )

    for k in range(2):
        part_copy(k, 1).start()

        @pl.when(p != 2 * odd + k)
        def _():
            part_copy(k, 0).start()

        @pl.when(p == 2 * odd + k)
        def _():
            pltpu.make_async_copy(part.at[k], pr.at[p], pr_recv).start()

    pltpu.make_async_copy(pr, pr, pr_recv).wait()
    ag2[mine] = (pr[0].astype(F32) + pr[1].astype(F32) + pr[2].astype(F32) + pr[3].astype(F32)).astype(BF16)
    sems2 = (ag2_send, ag2_z, ag2_recv)
    gather_start(ag2, sems2)
    gather_finish(ag2, sems2)
    solved = ag2[...].reshape(QUARTER, RHS)
    for q in range(4):
        lp[q] = mm(oh2[q * 128 : q * 128 + BOTH, :], solved).astype(BF16)
    lr[p] = lp[p]

    def look_copy(j, _):
        to = lax.rem(p + j, 4)
        pltpu.make_async_remote_copy(
            src_ref=lp.at[to], dst_ref=lr.at[p], send_sem=lk_send, recv_sem=lk_recv,
            device_id=(to, s), device_id_type=MESH,
        ).start()
        return 0

    lax.fori_loop(1, 4, look_copy, 0)
    pltpu.make_async_copy(lr.at[pl.ds(0, 3)], lr.at[pl.ds(0, 3)], lk_recv).wait()
    total = lr[0].astype(F32) + lr[1].astype(F32) + lr[2].astype(F32) + lr[3].astype(F32)
    looked[0:BOTH, :] = total.astype(BF16)

    for l in range(2):
        for m in range(3):
            rows = slice(m * FACE, (m + 1) * FACE)
            vec[l, rows, :] = (loc[l, rows, :] + mm(bt[l, rows, :], looked[...])).astype(BF16)
    exchange(1)

    permute_own(1)
    outs = []
    for l in range(2):
        arrived(1, l)
        for m in range(3):
            outv[l, :, m * FACE : (m + 1) * FACE] = permuted(1, l, m).T
        one = pltpu.make_async_copy(outv.at[l], out_h.at[l], out_sem.at[l])
        one.start()
        outs.append(one)

    for one in face_copies:
        one.wait_send()
    pltpu.make_async_copy(pm_all.at[pl.ds(0, 7)], pm_all.at[pl.ds(0, 7)], pm_send).wait()
    pltpu.make_async_copy(some, some, con_send).wait()
    for buf, sem, count in ((rpart, rs_send, 21), (zr, zr_send, 3), (ag1, ag1_send, 31), (ag2, ag2_send, 31)):
        sent = buf.at[pl.ds(0, count)]
        pltpu.make_async_copy(sent, sent, sem).wait()
    pltpu.make_async_copy(lr.at[pl.ds(0, 3)], lr.at[pl.ds(0, 3)], lk_send).wait()
    for k in range(2):
        part_copy(k, 1).wait_send()

        @pl.when(p != 2 * odd + k)
        def _():
            part_copy(k, 0).wait_send()

    for one in outs:
        one.wait()


def on_device(*operands):
    vmem, dma = pltpu.VMEM, pltpu.SemaphoreType.DMA
    return pl.pallas_call(
        kernel,
        out_shape=jax.ShapeDtypeStruct((2, RHS, IFACE), F32),
        in_specs=[pl.BlockSpec(memory_space=pl.ANY)] * 8,
        out_specs=pl.BlockSpec(memory_space=pl.ANY),
        scratch_shapes=[
            vmem((2, RHS, IFACE), BF16),
            vmem((2, IFACE, IFACE), BF16),
            vmem((2, 3, FACE, FACE), BF16),
            vmem((2, IFACE, IFACE), BF16),
            vmem((2, PRIM, IFACE), BF16),
            vmem((2, IFACE), I32),
            vmem((2, PRIM), I32),
            vmem((BOTH, QUARTER), F32),
            vmem((2, IFACE, IFACE), BF16),
            vmem((2, IFACE, IFACE), BF16),
            vmem((2, IFACE, IFACE), BF16),
            vmem((2, IFACE, RHS), BF16),
            vmem((2, IFACE, RHS), BF16),
            vmem((2, 2, 3, FACE, RHS), BF16),
            vmem((2, 2, 2, FACE, RHS), BF16),
            vmem((2, IFACE, RHS), F32),
            vmem((2, IFACE, RHS), BF16),
            vmem((2, IFACE, RHS), F32),
            vmem((2, 128, IFACE), F32),
            vmem((2, IFACE, 128), BF16),
            vmem((8, 128), I32),
            vmem((8, 8, 128), I32),
            vmem((8, 128, RHS), BF16),
            vmem((QUARTER, 1024), BF16),
            vmem((512, QUARTER), BF16),
            vmem((OWNERS, PIECE, RHS), BF16),
            vmem((3, 8, PIECE, RHS), BF16),
            vmem((2, PIECE, RHS), BF16),
            vmem((3, PIECE, RHS), BF16),
            vmem((OWNERS, PIECE, RHS), BF16),
            vmem((2, PIECE, RHS), BF16),
            vmem((4, PIECE, RHS), BF16),
            vmem((OWNERS, PIECE, RHS), BF16),
            vmem((4, BOTH, RHS), BF16),
            vmem((4, BOTH, RHS), BF16),
            vmem((128, RHS), BF16),
            vmem((2, RHS, IFACE), F32),
            dma((9,)), dma((2,)), dma((2, 2, 2)), dma((2, 2, 2)), dma, dma, dma, dma,
            dma, dma((3,)), dma, dma((3,)), dma, dma((3,)), dma, dma((2, 2)), dma, dma, dma((3,)), dma, dma, dma,
        ],
        compiler_params=pltpu.CompilerParams(
            collective_id=0, has_side_effects=True, vmem_limit_bytes=62 * 1024 * 1024
        ),
        cost_estimate=pl.CostEstimate(flops=3_000_000_000, bytes_accessed=9_000_000, transcendentals=0),
    )(*operands)


def solution(mesh):
    return jax.shard_map(
        on_device,
        mesh=mesh,
        in_specs=(
            P(("plane", "sub"), None, None),
            P(("plane", "sub"), None, None),
            P(("plane", "sub"), None, None, None),
            P(("plane", "sub"), None, None),
            P(("plane", "sub"), None, None),
            P(("plane", "sub"), None),
            P(("plane", "sub"), None),
            P("sub", None),
        ),
        out_specs=P(("plane", "sub"), None, None),
        check_vma=False,
    )
```

```python
import jax
import jax.numpy as jnp
from jax import lax
from jax.experimental import pallas as pl
from jax.experimental.pallas import tpu as pltpu
from jax.sharding import PartitionSpec as P

MESH = pl.DeviceIdType.MESH
F32, BF16, I32 = jnp.float32, jnp.bfloat16, jnp.int32
RHS, IFACE, FACE, PRIM = 128, 768, 256, 48
BOTH = 2 * PRIM
QUARTER = 1536
OWNERS = 32
PIECE = QUARTER // OWNERS


def mm(a, b):
    return jnp.dot(a, b, preferred_element_type=F32)


def onehot(mask):
    return jnp.where(mask, 1.0, 0.0).astype(BF16)


def column(row):
    return jnp.broadcast_to(row, (128, 128)).T


def kernel(
    res_h, schur_h, finv_h, linv_h, basis_h, fd_h, pm_h, cinv_h, own_h, other_h,
    res, schur, finv, linv, basis, fd, pm, cinv,
    pt, pp, sp, img, vec, w, got, acc, avg, loc, bpad, bt,
    pm_row, pm_all, con, oh1, oh2, rpart, rs, zs, zr, ag1, part, pr, ag2, lp, lr, looked, own, other,
    load_sem, out_sem, face_send, face_recv, pm_send, pm_recv, con_send, con_recv,
    rs_send, rs_recv, zr_send, zr_recv, ag1_send, ag1_z, ag1_recv, pr_send, pr_recv,
    ag2_send, ag2_z, ag2_recv, lk_send, lk_recv,
):
    p, s = lax.axis_index("plane"), lax.axis_index("sub")
    x, z, y = lax.div(s, 32), lax.rem(lax.div(s, 4), 8), lax.rem(s, 4)
    pair, odd = lax.div(z, 2), lax.rem(z, 2)
    sign = 2 * odd - 1
    xy = x * 4 + y
    mine = pair * 8 + xy

    def at(ax, az, ay):
        return lax.rem(ax, 2) * 32 + lax.rem(az, 8) * 4 + lax.rem(ay, 4)

    def along(j):
        return p, at(x, z + 8 + sign * j, y)

    def source(j):
        return lax.rem(z + 8 + (sign * j if j % 2 else -sign * j), 8)

    def across(i):
        return p, at(x + lax.div(i, 4), z, y + lax.rem(i, 4))

    def near(j):
        return lax.rem(p + lax.rem(j, 4), 4), at(x, z + 8 - sign * lax.div(j, 4), y)

    up, down = lax.rem(s + 1, 64), lax.rem(s + 63, 64)
    core = p + 1 - 2 * lax.rem(p, 2)
    far = p + 2 - 4 * lax.div(p, 2)

    def load(i, src, dst):
        return pltpu.make_async_copy(src, dst, load_sem.at[i])

    loads = [
        load(0, fd_h, fd),
        load(1, pm_h, pm),
        load(2, res_h, res),
        load(3, schur_h.at[0], schur.at[0]),
        load(4, schur_h.at[1], schur.at[1]),
        load(5, finv_h, finv),
        load(6, basis_h, basis),
        load(7, linv_h, linv),
        load(8, cinv_h.at[:, pl.ds(pl.multiple_of(p * QUARTER, QUARTER), QUARTER)], cinv),
    ]
    for one in loads:
        one.start()

    con[...] = jnp.zeros_like(con)
    looked[...] = jnp.zeros_like(looked)
    barrier = pltpu.get_barrier_semaphore()

    def greet(to):
        pl.semaphore_signal(barrier, inc=1, device_id=to, device_id_type=MESH)

    def greet_across(i, _):
        greet(across(i))
        return 0

    def greet_near(j, _):
        greet(near(j))
        return 0

    for j in (1, 2, 3):
        greet((p, at(x, source(j), y)))
    lax.fori_loop(1, 8, greet_across, 0)
    lax.fori_loop(1, 8, greet_near, 0)
    greet((p, up))
    greet((p, down))

    loads[1].wait()
    pm_row[...] = jnp.full((8, 128), -1, I32)
    pm_row[0:2, 0:PRIM] = pm[...]
    first = pm_row[0:1, :]
    second = pltpu.roll(jnp.broadcast_to(pm_row[1:2, :], (8, 128)), PRIM, 1)
    lane = lax.broadcasted_iota(I32, (8, 128), 1)
    pm_row[...] = jnp.where(lane < PRIM, jnp.broadcast_to(first, (8, 128)), jnp.where(lane < BOTH, second, -1))
    slot = odd * 4 + p
    pm_all[slot] = pm_row[...]

    def image(l):
        for m in range(3):
            rows = slice(m * FACE, (m + 1) * FACE)
            img[l, rows, :] = lax.dot_general(
                schur[l, rows, :], res[l], (((1,), (1,)), ((), ())), preferred_element_type=F32
            ).astype(BF16)

    def build_pp(l):
        row = fd[l : l + 1, :].astype(F32)
        for b in range(6):
            col = column(row[:, b * 128 : (b + 1) * 128])
            for c in range(6):
                lanes = lax.broadcasted_iota(I32, (128, 128), 1).astype(F32) + float(c * 128)
                pp[l, b * 128 : (b + 1) * 128, c * 128 : (c + 1) * 128] = onehot(col == lanes)

    def weigh(d, l, k):
        rows = slice(k * FACE, (k + 1) * FACE)
        if d == 0:
            faces = mm(pp[l, rows, :], img[l])
        else:
            faces = mm(sp[l, rows, :], vec[l])
        w[d, l, k] = mm(finv[l, k], faces.astype(BF16)).astype(BF16)

    def prepare(l):
        for k in range(3):
            rows = slice(k * FACE, (k + 1) * FACE)
            sp[l, rows, :] = mm(pp[l, rows, :], schur[l]).astype(BF16)

    def face_copy(d, l, k):
        if k == 1:
            to, there = (p, down if l == 0 else up), 1 - l
        else:
            to, there = (core if l == 0 else far, s), l
        return pltpu.make_async_remote_copy(
            src_ref=w.at[d, l, k],
            dst_ref=got.at[d, there, k - 1],
            send_sem=face_send.at[d, l, k - 1],
            recv_sem=face_recv.at[d, there, k - 1],
            device_id=to,
            device_id_type=MESH,
        )

    def arrived(d, l):
        for k in range(2):
            pltpu.make_async_copy(got.at[d, l, k], got.at[d, l, k], face_recv.at[d, l, k]).wait()

    def permute_own():
        for l in range(2):
            for m in range(3):
                rows = slice(m * FACE, (m + 1) * FACE)
                acc[l, rows, :] = mm(pt[l, rows, :], w[0, l].reshape(IFACE, RHS)) + mm(
                    pt[l, rows, 0:FACE], w[0, 1 - l, 0]
                )

    def permuted(d, l, m):
        rows = slice(m * FACE, (m + 1) * FACE)
        return acc[l, rows, :] + mm(pt[l, rows, FACE:], got[d, l].reshape(2 * FACE, RHS))

    face_copies = []

    def exchange(d):
        for l in range(2):
            if d == 0:
                loads[3 + l].wait()
                image(l)
                build_pp(l)
                if l == 0:
                    loads[5].wait()
            else:
                for m in range(3):
                    rows = slice(m * FACE, (m + 1) * FACE)
                    vec[l, rows, :] = (loc[l, rows, :] + mm(bt[l, rows, :], looked[...])).astype(BF16)
            for k in (1, 2):
                weigh(d, l, k)
                if d == 0 and l == 0 and k == 1:
                    pl.semaphore_wait(barrier, 3 + 7 + 7 + 2)
                    lax.fori_loop(1, 8, send_pm, 0)
                one = face_copy(d, l, k)
                one.start()
                face_copies.append(one)
        for l in range(2):
            weigh(d, l, 0)

    def send_pm(j, _):
        pltpu.make_async_remote_copy(
            src_ref=pm_row, dst_ref=pm_all.at[slot], send_sem=pm_send, recv_sem=pm_recv,
            device_id=near(j), device_id_type=MESH,
        ).start()
        return 0

    loads[0].wait()
    loads[2].wait()
    exchange(0)

    for l in range(2):
        row = fd[l : l + 1, :].astype(F32)
        for m in range(3):
            rows = lax.broadcasted_iota(I32, (FACE, IFACE), 0).astype(F32) + float(m * FACE)
            pt[l, m * FACE : (m + 1) * FACE, :] = onehot(rows == row)
    permute_own()
    loads[6].wait()
    bpad[...] = jnp.zeros_like(bpad)
    for l in range(2):
        bpad[l, l * PRIM : (l + 1) * PRIM, :] = basis[l].astype(F32)
        for b in range(6):
            bt[l, b * 128 : (b + 1) * 128, :] = bpad[l, :, b * 128 : (b + 1) * 128].T.astype(BF16)
    pltpu.make_async_copy(pm_all.at[pl.ds(0, 7)], pm_all.at[pl.ds(0, 7)], pm_recv).wait()
    for t in range(8):
        row = pm_all[t, 0:1, :].astype(F32) - (p * QUARTER).astype(F32)
        for m in range(6):
            rows = lax.broadcasted_iota(I32, (256, 128), 0).astype(F32) + float(m * 256)
            oh1[m * 256 : (m + 1) * 256, t * 128 : (t + 1) * 128] = onehot(rows == row)

    for l in range(2):
        arrived(0, l)
        for m in range(3):
            avg[l, m * FACE : (m + 1) * FACE, :] = permuted(0, l, m).astype(BF16)
        con[slot, l * PRIM : (l + 1) * PRIM, :] = mm(basis[l], avg[l]).astype(BF16)

        def send_con(j, _, l=l):
            half = con.at[slot, pl.ds(l * PRIM, PRIM)]
            pltpu.make_async_remote_copy(
                src_ref=half, dst_ref=half, send_sem=con_send.at[l], recv_sem=con_recv.at[l],
                device_id=near(j), device_id_type=MESH,
            ).start()
            return 0

        lax.fori_loop(1, 8, send_con, 0)

    loads[7].wait()
    for l in range(2):
        for m in range(3):
            loc[l, m * FACE : (m + 1) * FACE, :] = mm(linv[l, m * FACE : (m + 1) * FACE, :], avg[l])
    loads[8].wait()

    halves = con.at[pl.ds(0, 7), pl.ds(0, PRIM)]
    for l in range(2):
        pltpu.make_async_copy(halves, halves, con_recv.at[l]).wait()
    every = con[...].reshape(8 * 128, RHS)
    far_pair = lax.rem(pair + 2, 4)
    next_pair = lax.rem(pair + 4 + sign, 4)
    for n, target in enumerate((far_pair, next_pair, pair)):
        rows = oh1[pl.ds(pl.multiple_of(target * 8 * PIECE, 8 * PIECE), 8 * PIECE), :]
        rpart[n] = mm(rows, every).astype(BF16).reshape(8, PIECE, RHS)

        def send_rs(i, _, n=n):
            to = across(i)
            txy = lax.div(to[1], 32) * 4 + lax.rem(to[1], 4)
            pltpu.make_async_remote_copy(
                src_ref=rpart.at[n, txy], dst_ref=rs.at[n, xy], send_sem=rs_send, recv_sem=rs_recv.at[n],
                device_id=to, device_id_type=MESH,
            ).start()
            return 0

        lax.fori_loop(1, 8, send_rs, 0)
        rs[n, xy] = rpart[n, xy]

    for q in range(4):
        c = pm_all[odd * 4 + q].astype(F32)
        block = jnp.floor((c + 0.5) * (1.0 / 96.0))
        rem = c - 96.0 * block
        cx = jnp.floor((block + 0.5) * (1.0 / 32.0))
        cz = jnp.floor((block - 32.0 * cx + 0.5) * 0.25)
        cy = block - 32.0 * cx - 4.0 * cz
        cg = jnp.floor((cz + 0.5) * 0.5)
        ck = jnp.floor((rem + 0.5) * (1.0 / 48.0))
        owner = cg * 8.0 + cx * 4.0 + cy
        code = (2.0 * (cz - 2.0 * cg) + ck) * float(QUARTER) + owner * float(PIECE) + rem - 48.0 * ck
        code = jnp.where(c < 0.0, -1.0, code) - (p * QUARTER).astype(F32)
        col = column(code[0:1, :])
        for b in range(QUARTER // 128):
            lanes = lax.broadcasted_iota(I32, (128, 128), 1).astype(F32) + float(b * 128)
            oh2[q * 128 : (q + 1) * 128, b * 128 : (b + 1) * 128] = onehot(col == lanes)

    prepare(0)

    def z_copy(src, j, n):
        return pltpu.make_async_remote_copy(
            src_ref=src, dst_ref=zr.at[j - 1], send_sem=zr_send, recv_sem=zr_recv.at[j - 1],
            device_id=along(j), device_id_type=MESH,
        )

    for n in range(3):
        seven = rs.at[n, pl.ds(0, 7)]
        pltpu.make_async_copy(seven, seven, rs_recv.at[n]).wait()
        total = rs[n, 0].astype(F32)
        for i in range(1, 8):
            total = total + rs[n, i].astype(F32)
        if n < 2:
            zs[n] = total.astype(BF16)
            for j in ((3,), (2, 1))[n]:
                z_copy(zs.at[n], j, n).start()
    for j in (1, 2, 3):
        pltpu.make_async_copy(zr.at[j - 1], zr.at[j - 1], zr_recv.at[j - 1]).wait()
        total = total + zr[j - 1].astype(F32)

    def gather_start(buf, sems):
        send_sem, z_recv, xy_recv = sems
        own = buf.at[mine]
        for j in (3, 2, 1):
            pltpu.make_async_remote_copy(
                src_ref=own, dst_ref=own, send_sem=send_sem, recv_sem=z_recv.at[j - 1],
                device_id=along(j), device_id_type=MESH,
            ).start()
        relay(buf, mine, sems)

    def relay(buf, owner, sems):
        send_sem, _, xy_recv = sems
        piece = buf.at[owner]

        def send(i, _):
            pltpu.make_async_remote_copy(
                src_ref=piece, dst_ref=piece, send_sem=send_sem, recv_sem=xy_recv,
                device_id=across(i), device_id_type=MESH,
            ).start()
            return 0

        lax.fori_loop(1, 8, send, 0)

    def gather_finish(buf, sems):
        _, z_recv, xy_recv = sems
        for j in (1, 2, 3):
            owner = lax.div(source(j), 2) * 8 + xy
            pltpu.make_async_copy(buf.at[owner], buf.at[owner], z_recv.at[j - 1]).wait()
            relay(buf, owner, sems)
        pieces = buf.at[pl.ds(0, 28)]
        pltpu.make_async_copy(pieces, pieces, xy_recv).wait()

    ag1[mine] = total.astype(BF16)
    sems1 = (ag1_send, ag1_z, ag1_recv)
    gather_start(ag1, sems1)
    prepare(1)
    high = cinv[...].astype(BF16)
    low = (cinv[...] - high.astype(F32)).astype(BF16)
    gather_finish(ag1, sems1)
    residual = ag1[...].reshape(QUARTER, RHS)
    part[...] = (mm(high, residual) + mm(low, residual)).astype(BF16).reshape(2, PIECE, RHS)

    def part_copy(k, e):
        return pltpu.make_async_remote_copy(
            src_ref=part.at[k], dst_ref=pr.at[p], send_sem=pr_send.at[k, e], recv_sem=pr_recv,
            device_id=(2 * odd + k, at(x, z + 8 - sign * e, y)), device_id_type=MESH,
        )

    for k in range(2):
        part_copy(k, 1).start()

        @pl.when(p != 2 * odd + k)
        def _():
            part_copy(k, 0).start()

        @pl.when(p == 2 * odd + k)
        def _():
            pltpu.make_async_copy(part.at[k], pr.at[p], pr_recv).start()

    pltpu.make_async_copy(pr, pr, pr_recv).wait()
    ag2[mine] = (pr[0].astype(F32) + pr[1].astype(F32) + pr[2].astype(F32) + pr[3].astype(F32)).astype(BF16)
    sems2 = (ag2_send, ag2_z, ag2_recv)
    gather_start(ag2, sems2)
    gather_finish(ag2, sems2)
    solved = ag2[...].reshape(QUARTER, RHS)
    for j in (1, 2, 3, 0):
        to = lax.rem(p + j, 4)
        chosen = mm(oh2[pl.ds(pl.multiple_of(to * 128, 128), BOTH), :], solved).astype(BF16)
        if j == 0:
            lr[p] = chosen
        else:
            lp[j] = chosen
            pltpu.make_async_remote_copy(
                src_ref=lp.at[j], dst_ref=lr.at[p], send_sem=lk_send, recv_sem=lk_recv,
                device_id=(to, s), device_id_type=MESH,
            ).start()
    pltpu.make_async_copy(lr.at[pl.ds(0, 3)], lr.at[pl.ds(0, 3)], lk_recv).wait()
    total = lr[0].astype(F32) + lr[1].astype(F32) + lr[2].astype(F32) + lr[3].astype(F32)
    looked[0:BOTH, :] = total.astype(BF16)

    exchange(1)

    outs = []
    for l in range(2):
        for m in range(3):
            rows = slice(m * FACE, (m + 1) * FACE)
            own[l, :, rows] = mm(pt[l, rows, :], w[1, l].reshape(IFACE, RHS)).T.astype(BF16)
            acc[l, rows, :] = mm(pt[l, rows, 0:FACE], w[1, 1 - l, 0])
        one = pltpu.make_async_copy(own.at[l], own_h.at[l], out_sem.at[0, l])
        one.start()
        outs.append(one)
    for l in range(2):
        arrived(1, l)
        for m in range(3):
            other[l, :, m * FACE : (m + 1) * FACE] = permuted(1, l, m).T.astype(BF16)
        one = pltpu.make_async_copy(other.at[l], other_h.at[l], out_sem.at[1, l])
        one.start()
        outs.append(one)

    for one in face_copies:
        one.wait_send()
    pltpu.make_async_copy(pm_all.at[pl.ds(0, 7)], pm_all.at[pl.ds(0, 7)], pm_send).wait()
    for l in range(2):
        pltpu.make_async_copy(halves, halves, con_send.at[l]).wait()
    for buf, sem, count in ((ag1, rs_send, 21), (zr, zr_send, 3), (ag1, ag1_send, 31), (ag2, ag2_send, 31)):
        sent = buf.at[pl.ds(0, count)]
        pltpu.make_async_copy(sent, sent, sem).wait()
    pltpu.make_async_copy(lr.at[pl.ds(0, 3)], lr.at[pl.ds(0, 3)], lk_send).wait()
    for k in range(2):
        part_copy(k, 1).wait_send()

        @pl.when(p != 2 * odd + k)
        def _():
            part_copy(k, 0).wait_send()

    for one in outs:
        one.wait()


def on_device(*operands):
    vmem, dma = pltpu.VMEM, pltpu.SemaphoreType.DMA
    own, other = pl.pallas_call(
        kernel,
        out_shape=[jax.ShapeDtypeStruct((2, RHS, IFACE), BF16)] * 2,
        in_specs=[pl.BlockSpec(memory_space=pl.ANY)] * 8,
        out_specs=[pl.BlockSpec(memory_space=pl.ANY)] * 2,
        scratch_shapes=[
            vmem((2, RHS, IFACE), BF16),
            vmem((2, IFACE, IFACE), BF16),
            vmem((2, 3, FACE, FACE), BF16),
            vmem((2, IFACE, IFACE), BF16),
            vmem((2, PRIM, IFACE), BF16),
            vmem((2, IFACE), I32),
            vmem((2, PRIM), I32),
            vmem((BOTH, QUARTER), F32),
            vmem((2, IFACE, IFACE), BF16),
            vmem((2, IFACE, IFACE), BF16),
            vmem((2, IFACE, IFACE), BF16),
            vmem((2, IFACE, RHS), BF16),
            vmem((2, IFACE, RHS), BF16),
            vmem((2, 2, 3, FACE, RHS), BF16),
            vmem((2, 2, 2, FACE, RHS), BF16),
            vmem((2, IFACE, RHS), F32),
            vmem((2, IFACE, RHS), BF16),
            vmem((2, IFACE, RHS), F32),
            vmem((2, 128, IFACE), F32),
            vmem((2, IFACE, 128), BF16),
            vmem((8, 128), I32),
            vmem((8, 8, 128), I32),
            vmem((8, 128, RHS), BF16),
            vmem((QUARTER, 1024), BF16),
            vmem((512, QUARTER), BF16),
            vmem((3, 8, PIECE, RHS), BF16),
            vmem((3, 8, PIECE, RHS), BF16),
            vmem((2, PIECE, RHS), BF16),
            vmem((3, PIECE, RHS), BF16),
            vmem((OWNERS, PIECE, RHS), BF16),
            vmem((2, PIECE, RHS), BF16),
            vmem((4, PIECE, RHS), BF16),
            vmem((OWNERS, PIECE, RHS), BF16),
            vmem((4, BOTH, RHS), BF16),
            vmem((4, BOTH, RHS), BF16),
            vmem((128, RHS), BF16),
            vmem((2, RHS, IFACE), BF16),
            vmem((2, RHS, IFACE), BF16),
            dma((9,)), dma((2, 2)), dma((2, 2, 2)), dma((2, 2, 2)), dma, dma, dma((2,)), dma((2,)),
            dma, dma((3,)), dma, dma((3,)), dma, dma((3,)), dma, dma((2, 2)), dma, dma, dma((3,)), dma, dma, dma,
        ],
        compiler_params=pltpu.CompilerParams(
            collective_id=0, has_side_effects=True, vmem_limit_bytes=62 * 1024 * 1024
        ),
        cost_estimate=pl.CostEstimate(flops=3_000_000_000, bytes_accessed=9_000_000, transcendentals=0),
    )(*operands)
    return own.astype(F32) + other.astype(F32)


def solution(mesh):
    return jax.shard_map(
        on_device,
        mesh=mesh,
        in_specs=(
            P(("plane", "sub"), None, None),
            P(("plane", "sub"), None, None),
            P(("plane", "sub"), None, None, None),
            P(("plane", "sub"), None, None),
            P(("plane", "sub"), None, None),
            P(("plane", "sub"), None),
            P(("plane", "sub"), None),
            P("sub", None),
        ),
        out_specs=P(("plane", "sub"), None, None),
        check_vma=False,
    )
```

```python
import jax
import jax.numpy as jnp
from jax import lax
from jax.experimental import pallas as pl
from jax.experimental.pallas import tpu as pltpu
from jax.sharding import PartitionSpec as P

MESH = pl.DeviceIdType.MESH
F32, BF16, I32 = jnp.float32, jnp.bfloat16, jnp.int32
RHS, IFACE, FACE, PRIM = 128, 768, 256, 48
BOTH = 2 * PRIM
QUARTER = 1536
OWNERS = 32
PIECE = QUARTER // OWNERS


def mm(a, b):
    return jnp.dot(a, b, preferred_element_type=F32)


def onehot(mask):
    return jnp.where(mask, 1.0, 0.0).astype(BF16)


def column(row):
    return jnp.broadcast_to(row, (128, 128)).T


def kernel(
    res_h, schur_h, finv_h, linv_h, basis_h, fd_h, pm_h, cinv_h, own, other,
    res, schur, finv, linv, basis, fd, pm, cinv,
    pt, pp, sp, img, vec, w, got, acc, avg, loc, bpad, bt,
    pm_row, pm_all, con, oh1, oh2, rpart, rs, zs, zr, ag1, part, pr, ag2, lp, lr, looked,
    load_sem, face_send, face_recv, pm_send, pm_recv, con_send, con_recv,
    rs_send, rs_recv, zr_send, zr_recv, ag1_send, ag1_z, ag1_recv, pr_send, pr_recv,
    ag2_send, ag2_z, ag2_recv, lk_send, lk_recv,
):
    p, s = lax.axis_index("plane"), lax.axis_index("sub")
    x, z, y = lax.div(s, 32), lax.rem(lax.div(s, 4), 8), lax.rem(s, 4)
    pair, odd = lax.div(z, 2), lax.rem(z, 2)
    sign = 2 * odd - 1
    xy = x * 4 + y
    mine = pair * 8 + xy

    def at(ax, az, ay):
        return lax.rem(ax, 2) * 32 + lax.rem(az, 8) * 4 + lax.rem(ay, 4)

    def along(j):
        return p, at(x, z + 8 + sign * j, y)

    def source(j):
        return lax.rem(z + 8 + (sign * j if j % 2 else -sign * j), 8)

    def across(i):
        return p, at(x + lax.div(i, 4), z, y + lax.rem(i, 4))

    def near(j):
        return lax.rem(p + lax.rem(j, 4), 4), at(x, z + 8 - sign * lax.div(j, 4), y)

    up, down = lax.rem(s + 1, 64), lax.rem(s + 63, 64)
    core = p + 1 - 2 * lax.rem(p, 2)
    far = p + 2 - 4 * lax.div(p, 2)

    def load(i, src, dst):
        return pltpu.make_async_copy(src, dst, load_sem.at[i])

    loads = [
        load(0, fd_h, fd),
        load(1, pm_h, pm),
        load(2, res_h, res),
        load(3, schur_h.at[0], schur.at[0]),
        load(4, schur_h.at[1], schur.at[1]),
        load(5, finv_h, finv),
        load(6, basis_h, basis),
        load(7, linv_h, linv),
        load(8, cinv_h.at[:, pl.ds(pl.multiple_of(p * QUARTER, QUARTER), QUARTER)], cinv),
    ]
    for one in loads:
        one.start()

    con[...] = jnp.zeros_like(con)
    looked[...] = jnp.zeros_like(looked)
    barrier = pltpu.get_barrier_semaphore()

    def greet(to):
        pl.semaphore_signal(barrier, inc=1, device_id=to, device_id_type=MESH)

    def greet_across(i, _):
        greet(across(i))
        return 0

    def greet_near(j, _):
        greet(near(j))
        return 0

    for j in (1, 2, 3):
        greet((p, at(x, source(j), y)))
    lax.fori_loop(1, 8, greet_across, 0)
    lax.fori_loop(1, 8, greet_near, 0)
    greet((p, up))
    greet((p, down))

    loads[1].wait()
    pm_row[...] = jnp.full((8, 128), -1, I32)
    pm_row[0:2, 0:PRIM] = pm[...]
    first = pm_row[0:1, :]
    second = pltpu.roll(jnp.broadcast_to(pm_row[1:2, :], (8, 128)), PRIM, 1)
    lane = lax.broadcasted_iota(I32, (8, 128), 1)
    pm_row[...] = jnp.where(lane < PRIM, jnp.broadcast_to(first, (8, 128)), jnp.where(lane < BOTH, second, -1))
    slot = odd * 4 + p
    pm_all[slot] = pm_row[...]

    def image(l):
        for m in range(3):
            rows = slice(m * FACE, (m + 1) * FACE)
            img[l, rows, :] = lax.dot_general(
                schur[l, rows, :], res[l], (((1,), (1,)), ((), ())), preferred_element_type=F32
            ).astype(BF16)

    def build_pp(l):
        row = fd[l : l + 1, :].astype(F32)
        for b in range(6):
            col = column(row[:, b * 128 : (b + 1) * 128])
            for c in range(6):
                lanes = lax.broadcasted_iota(I32, (128, 128), 1).astype(F32) + float(c * 128)
                pp[l, b * 128 : (b + 1) * 128, c * 128 : (c + 1) * 128] = onehot(col == lanes)

    def weigh(d, l, k):
        rows = slice(k * FACE, (k + 1) * FACE)
        if d == 0:
            faces = mm(pp[l, rows, :], img[l])
        else:
            faces = mm(sp[l, rows, :], vec[l])
        w[d, l, k] = mm(finv[l, k], faces.astype(BF16)).astype(BF16)

    def prepare(l):
        for k in range(3):
            rows = slice(k * FACE, (k + 1) * FACE)
            sp[l, rows, :] = mm(pp[l, rows, :], schur[l]).astype(BF16)

    def face_copy(d, l, k):
        if k == 1:
            to, there = (p, down if l == 0 else up), 1 - l
        else:
            to, there = (core if l == 0 else far, s), l
        return pltpu.make_async_remote_copy(
            src_ref=w.at[d, l, k],
            dst_ref=got.at[d, there, k - 1],
            send_sem=face_send.at[d, l, k - 1],
            recv_sem=face_recv.at[d, there, k - 1],
            device_id=to,
            device_id_type=MESH,
        )

    def arrived(d, l):
        for k in range(2):
            pltpu.make_async_copy(got.at[d, l, k], got.at[d, l, k], face_recv.at[d, l, k]).wait()

    def permute_own():
        for l in range(2):
            for m in range(3):
                rows = slice(m * FACE, (m + 1) * FACE)
                acc[l, rows, :] = mm(pt[l, rows, :], w[0, l].reshape(IFACE, RHS)) + mm(
                    pt[l, rows, 0:FACE], w[0, 1 - l, 0]
                )

    def permuted(d, l, m):
        rows = slice(m * FACE, (m + 1) * FACE)
        return acc[l, rows, :] + mm(pt[l, rows, FACE:], got[d, l].reshape(2 * FACE, RHS))

    face_copies = []

    def exchange(d):
        for l in range(2):
            if d == 0:
                loads[3 + l].wait()
                image(l)
                build_pp(l)
                if l == 0:
                    loads[5].wait()
            else:
                for m in range(3):
                    rows = slice(m * FACE, (m + 1) * FACE)
                    vec[l, rows, :] = (loc[l, rows, :] + mm(bt[l, rows, :], looked[...])).astype(BF16)
            for k in (1, 2):
                weigh(d, l, k)
                if d == 0 and l == 0 and k == 1:
                    pl.semaphore_wait(barrier, 3 + 7 + 7 + 2)
                    lax.fori_loop(1, 8, send_pm, 0)
                one = face_copy(d, l, k)
                one.start()
                face_copies.append(one)
        for l in range(2):
            weigh(d, l, 0)

    def send_pm(j, _):
        pltpu.make_async_remote_copy(
            src_ref=pm_row, dst_ref=pm_all.at[slot], send_sem=pm_send, recv_sem=pm_recv,
            device_id=near(j), device_id_type=MESH,
        ).start()
        return 0

    loads[0].wait()
    loads[2].wait()
    exchange(0)

    for l in range(2):
        row = fd[l : l + 1, :].astype(F32)
        for m in range(3):
            rows = lax.broadcasted_iota(I32, (FACE, IFACE), 0).astype(F32) + float(m * FACE)
            pt[l, m * FACE : (m + 1) * FACE, :] = onehot(rows == row)
    permute_own()
    loads[6].wait()
    bpad[...] = jnp.zeros_like(bpad)
    for l in range(2):
        bpad[l, l * PRIM : (l + 1) * PRIM, :] = basis[l].astype(F32)
        for b in range(6):
            bt[l, b * 128 : (b + 1) * 128, :] = bpad[l, :, b * 128 : (b + 1) * 128].T.astype(BF16)
    pltpu.make_async_copy(pm_all.at[pl.ds(0, 7)], pm_all.at[pl.ds(0, 7)], pm_recv).wait()
    for t in range(8):
        row = pm_all[t, 0:1, :].astype(F32) - (p * QUARTER).astype(F32)
        for m in range(6):
            rows = lax.broadcasted_iota(I32, (256, 128), 0).astype(F32) + float(m * 256)
            oh1[m * 256 : (m + 1) * 256, t * 128 : (t + 1) * 128] = onehot(rows == row)

    for l in range(2):
        arrived(0, l)
        for m in range(3):
            avg[l, m * FACE : (m + 1) * FACE, :] = permuted(0, l, m).astype(BF16)
        con[slot, l * PRIM : (l + 1) * PRIM, :] = mm(basis[l], avg[l]).astype(BF16)

        def send_con(j, _, l=l):
            half = con.at[slot, pl.ds(l * PRIM, PRIM)]
            pltpu.make_async_remote_copy(
                src_ref=half, dst_ref=half, send_sem=con_send.at[l], recv_sem=con_recv.at[l],
                device_id=near(8 - j), device_id_type=MESH,
            ).start()
            return 0

        lax.fori_loop(1, 8, send_con, 0)

    loads[7].wait()
    for l in range(2):
        for m in range(3):
            loc[l, m * FACE : (m + 1) * FACE, :] = mm(linv[l, m * FACE : (m + 1) * FACE, :], avg[l])
    loads[8].wait()

    halves = con.at[pl.ds(0, 7), pl.ds(0, PRIM)]
    for l in range(2):
        pltpu.make_async_copy(halves, halves, con_recv.at[l]).wait()
    every = con[...].reshape(8 * 128, RHS)
    far_pair = lax.rem(pair + 2, 4)
    next_pair = lax.rem(pair + 4 + sign, 4)
    for n, target in enumerate((far_pair, next_pair, pair)):
        rows = oh1[pl.ds(pl.multiple_of(target * 8 * PIECE, 8 * PIECE), 8 * PIECE), :]
        rpart[n] = mm(rows, every).astype(BF16).reshape(8, PIECE, RHS)

        def send_rs(i, _, n=n):
            to = across(8 - i)
            txy = lax.div(to[1], 32) * 4 + lax.rem(to[1], 4)
            pltpu.make_async_remote_copy(
                src_ref=rpart.at[n, txy], dst_ref=rs.at[n, xy], send_sem=rs_send, recv_sem=rs_recv.at[n],
                device_id=to, device_id_type=MESH,
            ).start()
            return 0

        lax.fori_loop(1, 8, send_rs, 0)
        rs[n, xy] = rpart[n, xy]

    for q in range(4):
        c = pm_all[odd * 4 + q].astype(F32)
        block = jnp.floor((c + 0.5) * (1.0 / 96.0))
        rem = c - 96.0 * block
        cx = jnp.floor((block + 0.5) * (1.0 / 32.0))
        cz = jnp.floor((block - 32.0 * cx + 0.5) * 0.25)
        cy = block - 32.0 * cx - 4.0 * cz
        cg = jnp.floor((cz + 0.5) * 0.5)
        ck = jnp.floor((rem + 0.5) * (1.0 / 48.0))
        owner = cg * 8.0 + cx * 4.0 + cy
        code = (2.0 * (cz - 2.0 * cg) + ck) * float(QUARTER) + owner * float(PIECE) + rem - 48.0 * ck
        code = jnp.where(c < 0.0, -1.0, code) - (p * QUARTER).astype(F32)
        col = column(code[0:1, :])
        for b in range(QUARTER // 128):
            lanes = lax.broadcasted_iota(I32, (128, 128), 1).astype(F32) + float(b * 128)
            oh2[q * 128 : (q + 1) * 128, b * 128 : (b + 1) * 128] = onehot(col == lanes)

    prepare(0)
    prepare(1)

    def z_copy(src, j, n):
        return pltpu.make_async_remote_copy(
            src_ref=src, dst_ref=zr.at[j - 1], send_sem=zr_send, recv_sem=zr_recv.at[j - 1],
            device_id=along(j), device_id_type=MESH,
        )

    for n in range(3):
        seven = rs.at[n, pl.ds(0, 7)]
        pltpu.make_async_copy(seven, seven, rs_recv.at[n]).wait()
        total = rs[n, 0].astype(F32)
        for i in range(1, 8):
            total = total + rs[n, i].astype(F32)
        if n < 2:
            zs[n] = total.astype(BF16)
            for j in ((3,), (2, 1))[n]:
                z_copy(zs.at[n], j, n).start()
    for j in (1, 2, 3):
        pltpu.make_async_copy(zr.at[j - 1], zr.at[j - 1], zr_recv.at[j - 1]).wait()
        total = total + zr[j - 1].astype(F32)

    def gather_start(buf, sems):
        send_sem, z_recv, xy_recv = sems
        own = buf.at[mine]
        for j in (3, 2, 1):
            pltpu.make_async_remote_copy(
                src_ref=own, dst_ref=own, send_sem=send_sem, recv_sem=z_recv.at[j - 1],
                device_id=along(j), device_id_type=MESH,
            ).start()
        relay(buf, mine, sems)

    def relay(buf, owner, sems):
        send_sem, _, xy_recv = sems
        piece = buf.at[owner]

        def send(i, _):
            pltpu.make_async_remote_copy(
                src_ref=piece, dst_ref=piece, send_sem=send_sem, recv_sem=xy_recv,
                device_id=across(8 - i), device_id_type=MESH,
            ).start()
            return 0

        lax.fori_loop(1, 8, send, 0)

    def gather_finish(buf, sems):
        _, z_recv, xy_recv = sems
        for j in (1, 2, 3):
            owner = lax.div(source(j), 2) * 8 + xy
            pltpu.make_async_copy(buf.at[owner], buf.at[owner], z_recv.at[j - 1]).wait()
            relay(buf, owner, sems)
        pieces = buf.at[pl.ds(0, 28)]
        pltpu.make_async_copy(pieces, pieces, xy_recv).wait()

    ag1[mine] = total.astype(BF16)
    sems1 = (ag1_send, ag1_z, ag1_recv)
    gather_start(ag1, sems1)
    high = cinv[...].astype(BF16)
    low = (cinv[...] - high.astype(F32)).astype(BF16)
    gather_finish(ag1, sems1)
    residual = ag1[...].reshape(QUARTER, RHS)
    part[...] = (mm(high, residual) + mm(low, residual)).astype(BF16).reshape(2, PIECE, RHS)

    def part_copy(k, e):
        return pltpu.make_async_remote_copy(
            src_ref=part.at[k], dst_ref=pr.at[p], send_sem=pr_send.at[k, e], recv_sem=pr_recv,
            device_id=(2 * odd + k, at(x, z + 8 - sign * e, y)), device_id_type=MESH,
        )

    for k in range(2):
        part_copy(k, 1).start()

        @pl.when(p != 2 * odd + k)
        def _():
            part_copy(k, 0).start()

        @pl.when(p == 2 * odd + k)
        def _():
            pltpu.make_async_copy(part.at[k], pr.at[p], pr_recv).start()

    pltpu.make_async_copy(pr, pr, pr_recv).wait()
    ag2[mine] = (pr[0].astype(F32) + pr[1].astype(F32) + pr[2].astype(F32) + pr[3].astype(F32)).astype(BF16)
    sems2 = (ag2_send, ag2_z, ag2_recv)
    gather_start(ag2, sems2)
    gather_finish(ag2, sems2)
    solved = ag2[...].reshape(QUARTER, RHS)
    for j in (1, 2, 3, 0):
        to = lax.rem(p + j, 4)
        chosen = mm(oh2[pl.ds(pl.multiple_of(to * 128, 128), BOTH), :], solved).astype(BF16)
        if j == 0:
            lr[p] = chosen
        else:
            lp[j] = chosen
            pltpu.make_async_remote_copy(
                src_ref=lp.at[j], dst_ref=lr.at[p], send_sem=lk_send, recv_sem=lk_recv,
                device_id=(to, s), device_id_type=MESH,
            ).start()
    pltpu.make_async_copy(lr.at[pl.ds(0, 3)], lr.at[pl.ds(0, 3)], lk_recv).wait()
    total = lr[0].astype(F32) + lr[1].astype(F32) + lr[2].astype(F32) + lr[3].astype(F32)
    looked[0:BOTH, :] = total.astype(BF16)

    exchange(1)

    for l in range(2):
        for m in range(3):
            rows = slice(m * FACE, (m + 1) * FACE)
            own[l, :, rows] = mm(pt[l, rows, :], w[1, l].reshape(IFACE, RHS)).T.astype(BF16)
            acc[l, rows, :] = mm(pt[l, rows, 0:FACE], w[1, 1 - l, 0])
    for l in range(2):
        arrived(1, l)
        for m in range(3):
            other[l, :, m * FACE : (m + 1) * FACE] = permuted(1, l, m).T.astype(BF16)

    for one in face_copies:
        one.wait_send()
    pltpu.make_async_copy(pm_all.at[pl.ds(0, 7)], pm_all.at[pl.ds(0, 7)], pm_send).wait()
    for l in range(2):
        pltpu.make_async_copy(halves, halves, con_send.at[l]).wait()
    for buf, sem, count in ((ag1, rs_send, 21), (zr, zr_send, 3), (ag1, ag1_send, 31), (ag2, ag2_send, 31)):
        sent = buf.at[pl.ds(0, count)]
        pltpu.make_async_copy(sent, sent, sem).wait()
    pltpu.make_async_copy(lr.at[pl.ds(0, 3)], lr.at[pl.ds(0, 3)], lk_send).wait()
    for k in range(2):
        part_copy(k, 1).wait_send()

        @pl.when(p != 2 * odd + k)
        def _():
            part_copy(k, 0).wait_send()


def on_device(*operands):
    vmem, dma = pltpu.VMEM, pltpu.SemaphoreType.DMA
    operands = [pltpu.with_memory_space_constraint(one, pltpu.HBM) for one in operands]
    own, other = pl.pallas_call(
        kernel,
        out_shape=[jax.ShapeDtypeStruct((2, RHS, IFACE), BF16)] * 2,
        in_specs=[pl.BlockSpec(memory_space=pl.ANY)] * 8,
        out_specs=[pl.BlockSpec(memory_space=pltpu.VMEM)] * 2,
        scratch_shapes=[
            vmem((2, RHS, IFACE), BF16),
            vmem((2, IFACE, IFACE), BF16),
            vmem((2, 3, FACE, FACE), BF16),
            vmem((2, IFACE, IFACE), BF16),
            vmem((2, PRIM, IFACE), BF16),
            vmem((2, IFACE), I32),
            vmem((2, PRIM), I32),
            vmem((BOTH, QUARTER), F32),
            vmem((2, IFACE, IFACE), BF16),
            vmem((2, IFACE, IFACE), BF16),
            vmem((2, IFACE, IFACE), BF16),
            vmem((2, IFACE, RHS), BF16),
            vmem((2, IFACE, RHS), BF16),
            vmem((2, 2, 3, FACE, RHS), BF16),
            vmem((2, 2, 2, FACE, RHS), BF16),
            vmem((2, IFACE, RHS), F32),
            vmem((2, IFACE, RHS), BF16),
            vmem((2, IFACE, RHS), F32),
            vmem((2, 128, IFACE), F32),
            vmem((2, IFACE, 128), BF16),
            vmem((8, 128), I32),
            vmem((8, 8, 128), I32),
            vmem((8, 128, RHS), BF16),
            vmem((QUARTER, 1024), BF16),
            vmem((512, QUARTER), BF16),
            vmem((3, 8, PIECE, RHS), BF16),
            vmem((3, 8, PIECE, RHS), BF16),
            vmem((2, PIECE, RHS), BF16),
            vmem((3, PIECE, RHS), BF16),
            vmem((OWNERS, PIECE, RHS), BF16),
            vmem((2, PIECE, RHS), BF16),
            vmem((4, PIECE, RHS), BF16),
            vmem((OWNERS, PIECE, RHS), BF16),
            vmem((4, BOTH, RHS), BF16),
            vmem((4, BOTH, RHS), BF16),
            vmem((128, RHS), BF16),
            dma((9,)), dma((2, 2, 2)), dma((2, 2, 2)), dma, dma, dma((2,)), dma((2,)),
            dma, dma((3,)), dma, dma((3,)), dma, dma((3,)), dma, dma((2, 2)), dma, dma, dma((3,)), dma, dma, dma,
        ],
        compiler_params=pltpu.CompilerParams(
            collective_id=0, has_side_effects=True, vmem_limit_bytes=48 * 1024 * 1024
        ),
        cost_estimate=pl.CostEstimate(flops=3_000_000_000, bytes_accessed=9_000_000, transcendentals=0),
    )(*operands)
    return own.astype(F32) + other.astype(F32)


def solution(mesh):
    return jax.shard_map(
        on_device,
        mesh=mesh,
        in_specs=(
            P(("plane", "sub"), None, None),
            P(("plane", "sub"), None, None),
            P(("plane", "sub"), None, None, None),
            P(("plane", "sub"), None, None),
            P(("plane", "sub"), None, None),
            P(("plane", "sub"), None),
            P(("plane", "sub"), None),
            P("sub", None),
        ),
        out_specs=P(("plane", "sub"), None, None),
        check_vma=False,
    )
```

```python
import jax
import jax.numpy as jnp
from jax import lax
from jax.experimental import pallas as pl
from jax.experimental.pallas import tpu as pltpu
from jax.sharding import PartitionSpec as P

MESH = pl.DeviceIdType.MESH
F32, BF16, I32 = jnp.float32, jnp.bfloat16, jnp.int32
RHS, IFACE, FACE, PRIM = 128, 768, 256, 48
BOTH = 2 * PRIM
QUARTER = 1536
OWNERS = 32
PIECE = QUARTER // OWNERS


def mm(a, b):
    return jnp.dot(a, b, preferred_element_type=F32)


def onehot(mask):
    return jnp.where(mask, 1.0, 0.0).astype(BF16)


def column(row):
    return jnp.broadcast_to(row, (128, 128)).T


def kernel(
    res_h, schur_h, finv_h, linv_h, basis_h, fd_h, pm_h, cinv_h, own, other,
    res, schur, finv, linv, basis, fd, pm, cinv,
    pt, pp, sp, img, vec, w, got, acc, avg, loc, bpad, bt,
    pm_row, pm_all, con, oh1, oh2, rpart, rs, zs, zr, ag1, part, pr, ag2, lp, lr, looked,
    load_sem, face_send, face_recv, pm_send, pm_recv, con_send, con_recv,
    rs_send, rs_recv, zr_send, zr_recv, ag1_send, ag1_z, ag1_recv, pr_send, pr_recv,
    ag2_send, ag2_z, ag2_recv, lk_send, lk_recv,
):
    p, s = lax.axis_index("plane"), lax.axis_index("sub")
    x, z, y = lax.div(s, 32), lax.rem(lax.div(s, 4), 8), lax.rem(s, 4)
    pair, odd = lax.div(z, 2), lax.rem(z, 2)
    sign = 2 * odd - 1
    xy = x * 4 + y
    mine = pair * 8 + xy

    def at(ax, az, ay):
        return lax.rem(ax, 2) * 32 + lax.rem(az, 8) * 4 + lax.rem(ay, 4)

    def along(j):
        return p, at(x, z + 8 + sign * j, y)

    def source(j):
        return lax.rem(z + 8 + (sign * j if j % 2 else -sign * j), 8)

    def beyond(i):
        return p, at(x + lax.div(i, 4), z + 8 + 3 * sign, y + lax.rem(i, 4))

    def across(i):
        return p, at(x + lax.div(i, 4), z, y + lax.rem(i, 4))

    def near(j):
        return lax.rem(p + lax.rem(j, 4), 4), at(x, z + 8 - sign * lax.div(j, 4), y)

    up, down = lax.rem(s + 1, 64), lax.rem(s + 63, 64)
    core = p + 1 - 2 * lax.rem(p, 2)
    far = p + 2 - 4 * lax.div(p, 2)

    def load(i, src, dst):
        return pltpu.make_async_copy(src, dst, load_sem.at[i])

    loads = [
        load(0, fd_h, fd),
        load(1, pm_h, pm),
        load(2, res_h, res),
        load(3, schur_h.at[0], schur.at[0]),
        load(4, schur_h.at[1], schur.at[1]),
        load(5, finv_h, finv),
        load(6, basis_h, basis),
        load(7, linv_h, linv),
        load(8, cinv_h.at[:, pl.ds(pl.multiple_of(p * QUARTER, QUARTER), QUARTER)], cinv),
    ]
    for one in loads:
        one.start()

    con[...] = jnp.zeros_like(con)
    looked[...] = jnp.zeros_like(looked)
    barrier = pltpu.get_barrier_semaphore()

    def greet(to):
        pl.semaphore_signal(barrier, inc=1, device_id=to, device_id_type=MESH)

    def greet_across(i, _):
        greet(across(i))
        return 0

    def greet_near(j, _):
        greet(near(j))
        return 0

    def greet_beyond(i, _):
        greet(beyond(i))
        return 0

    for j in (1, 2):
        greet((p, at(x, source(j), y)))
    lax.fori_loop(0, 8, greet_beyond, 0)
    lax.fori_loop(1, 8, greet_across, 0)
    lax.fori_loop(1, 8, greet_near, 0)
    greet((p, up))
    greet((p, down))

    loads[1].wait()
    pm_row[...] = jnp.full((8, 128), -1, I32)
    pm_row[0:2, 0:PRIM] = pm[...]
    first = pm_row[0:1, :]
    second = pltpu.roll(jnp.broadcast_to(pm_row[1:2, :], (8, 128)), PRIM, 1)
    lane = lax.broadcasted_iota(I32, (8, 128), 1)
    pm_row[...] = jnp.where(lane < PRIM, jnp.broadcast_to(first, (8, 128)), jnp.where(lane < BOTH, second, -1))
    slot = odd * 4 + p
    pm_all[slot] = pm_row[...]

    def image(l):
        for m in range(3):
            rows = slice(m * FACE, (m + 1) * FACE)
            img[l, rows, :] = lax.dot_general(
                schur[l, rows, :], res[l], (((1,), (1,)), ((), ())), preferred_element_type=F32
            ).astype(BF16)

    def build_pp(l):
        row = fd[l : l + 1, :].astype(F32)
        for b in range(6):
            col = column(row[:, b * 128 : (b + 1) * 128])
            for c in range(6):
                lanes = lax.broadcasted_iota(I32, (128, 128), 1).astype(F32) + float(c * 128)
                pp[l, b * 128 : (b + 1) * 128, c * 128 : (c + 1) * 128] = onehot(col == lanes)

    def weigh(d, l, k):
        rows = slice(k * FACE, (k + 1) * FACE)
        if d == 0:
            faces = mm(pp[l, rows, :], img[l])
        else:
            faces = mm(sp[l, rows, :], vec[l])
        w[d, l, k] = mm(finv[l, k], faces.astype(BF16)).astype(BF16)

    def prepare(l):
        for k in range(3):
            rows = slice(k * FACE, (k + 1) * FACE)
            sp[l, rows, :] = mm(pp[l, rows, :], schur[l]).astype(BF16)

    def face_copy(d, l, k):
        if k == 1:
            to, there = (p, down if l == 0 else up), 1 - l
        else:
            to, there = (core if l == 0 else far, s), l
        return pltpu.make_async_remote_copy(
            src_ref=w.at[d, l, k],
            dst_ref=got.at[d, there, k - 1],
            send_sem=face_send.at[d, l, k - 1],
            recv_sem=face_recv.at[d, there, k - 1],
            device_id=to,
            device_id_type=MESH,
        )

    def arrived(d, l):
        for k in range(2):
            pltpu.make_async_copy(got.at[d, l, k], got.at[d, l, k], face_recv.at[d, l, k]).wait()

    def permute_own():
        for l in range(2):
            for m in range(3):
                rows = slice(m * FACE, (m + 1) * FACE)
                acc[l, rows, :] = mm(pt[l, rows, :], w[0, l].reshape(IFACE, RHS)) + mm(
                    pt[l, rows, 0:FACE], w[0, 1 - l, 0]
                )

    def permuted(d, l, m):
        rows = slice(m * FACE, (m + 1) * FACE)
        return acc[l, rows, :] + mm(pt[l, rows, FACE:], got[d, l].reshape(2 * FACE, RHS))

    face_copies = []

    def exchange(d):
        for l in range(2):
            if d == 0:
                loads[3 + l].wait()
                image(l)
                build_pp(l)
                if l == 0:
                    loads[5].wait()
            else:
                for m in range(3):
                    rows = slice(m * FACE, (m + 1) * FACE)
                    vec[l, rows, :] = (loc[l, rows, :] + mm(bt[l, rows, :], looked[...])).astype(BF16)
            for k in (1, 2):
                weigh(d, l, k)
                if d == 0 and l == 0 and k == 1:
                    pl.semaphore_wait(barrier, 2 + 8 + 7 + 7 + 2)
                    lax.fori_loop(1, 8, send_pm, 0)
                one = face_copy(d, l, k)
                one.start()
                face_copies.append(one)
        for l in range(2):
            weigh(d, l, 0)

    def send_pm(j, _):
        pltpu.make_async_remote_copy(
            src_ref=pm_row, dst_ref=pm_all.at[slot], send_sem=pm_send, recv_sem=pm_recv,
            device_id=near(j), device_id_type=MESH,
        ).start()
        return 0

    loads[0].wait()
    loads[2].wait()
    exchange(0)

    for l in range(2):
        row = fd[l : l + 1, :].astype(F32)
        for m in range(3):
            rows = lax.broadcasted_iota(I32, (FACE, IFACE), 0).astype(F32) + float(m * FACE)
            pt[l, m * FACE : (m + 1) * FACE, :] = onehot(rows == row)
    permute_own()
    loads[6].wait()
    bpad[...] = jnp.zeros_like(bpad)
    for l in range(2):
        bpad[l, l * PRIM : (l + 1) * PRIM, :] = basis[l].astype(F32)
        for b in range(6):
            bt[l, b * 128 : (b + 1) * 128, :] = bpad[l, :, b * 128 : (b + 1) * 128].T.astype(BF16)
    pltpu.make_async_copy(pm_all.at[pl.ds(0, 7)], pm_all.at[pl.ds(0, 7)], pm_recv).wait()
    for t in range(8):
        row = pm_all[t, 0:1, :].astype(F32) - (p * QUARTER).astype(F32)
        for m in range(6):
            rows = lax.broadcasted_iota(I32, (256, 128), 0).astype(F32) + float(m * 256)
            oh1[m * 256 : (m + 1) * 256, t * 128 : (t + 1) * 128] = onehot(rows == row)

    for l in range(2):
        arrived(0, l)
        for m in range(3):
            avg[l, m * FACE : (m + 1) * FACE, :] = permuted(0, l, m).astype(BF16)
        con[slot, l * PRIM : (l + 1) * PRIM, :] = mm(basis[l], avg[l]).astype(BF16)

        def send_con(j, _, l=l):
            half = con.at[slot, pl.ds(l * PRIM, PRIM)]
            pltpu.make_async_remote_copy(
                src_ref=half, dst_ref=half, send_sem=con_send.at[l], recv_sem=con_recv.at[l],
                device_id=near(8 - j), device_id_type=MESH,
            ).start()
            return 0

        lax.fori_loop(1, 8, send_con, 0)

    loads[7].wait()
    for l in range(2):
        for m in range(3):
            loc[l, m * FACE : (m + 1) * FACE, :] = mm(linv[l, m * FACE : (m + 1) * FACE, :], avg[l])
    loads[8].wait()

    halves = con.at[pl.ds(0, 7), pl.ds(0, PRIM)]
    for l in range(2):
        pltpu.make_async_copy(halves, halves, con_recv.at[l]).wait()
    every = con[...].reshape(8 * 128, RHS)
    far_pair = lax.rem(pair + 2, 4)
    next_pair = lax.rem(pair + 4 + sign, 4)
    for n, target in enumerate((far_pair, next_pair, pair)):
        rows = oh1[pl.ds(pl.multiple_of(target * 8 * PIECE, 8 * PIECE), 8 * PIECE), :]
        rpart[n] = mm(rows, every).astype(BF16).reshape(8, PIECE, RHS)

        def send_rs(i, _, n=n):
            to = across(8 - i)
            txy = lax.div(to[1], 32) * 4 + lax.rem(to[1], 4)
            pltpu.make_async_remote_copy(
                src_ref=rpart.at[n, txy], dst_ref=rs.at[n, xy], send_sem=rs_send, recv_sem=rs_recv.at[n],
                device_id=to, device_id_type=MESH,
            ).start()
            return 0

        lax.fori_loop(1, 8, send_rs, 0)
        rs[n, xy] = rpart[n, xy]

    for q in range(4):
        c = pm_all[odd * 4 + q].astype(F32)
        block = jnp.floor((c + 0.5) * (1.0 / 96.0))
        rem = c - 96.0 * block
        cx = jnp.floor((block + 0.5) * (1.0 / 32.0))
        cz = jnp.floor((block - 32.0 * cx + 0.5) * 0.25)
        cy = block - 32.0 * cx - 4.0 * cz
        cg = jnp.floor((cz + 0.5) * 0.5)
        ck = jnp.floor((rem + 0.5) * (1.0 / 48.0))
        owner = cg * 8.0 + cx * 4.0 + cy
        code = (2.0 * (cz - 2.0 * cg) + ck) * float(QUARTER) + owner * float(PIECE) + rem - 48.0 * ck
        code = jnp.where(c < 0.0, -1.0, code) - (p * QUARTER).astype(F32)
        col = column(code[0:1, :])
        for b in range(QUARTER // 128):
            lanes = lax.broadcasted_iota(I32, (128, 128), 1).astype(F32) + float(b * 128)
            oh2[q * 128 : (q + 1) * 128, b * 128 : (b + 1) * 128] = onehot(col == lanes)

    prepare(0)
    prepare(1)

    def z_copy(src, j, n):
        return pltpu.make_async_remote_copy(
            src_ref=src, dst_ref=zr.at[j - 1], send_sem=zr_send, recv_sem=zr_recv.at[j - 1],
            device_id=along(j), device_id_type=MESH,
        )

    for n in range(3):
        seven = rs.at[n, pl.ds(0, 7)]
        pltpu.make_async_copy(seven, seven, rs_recv.at[n]).wait()
        total = rs[n, 0].astype(F32)
        for i in range(1, 8):
            total = total + rs[n, i].astype(F32)
        if n < 2:
            zs[n] = total.astype(BF16)
            for j in ((3,), (2, 1))[n]:
                z_copy(zs.at[n], j, n).start()
    for j in (1, 2, 3):
        pltpu.make_async_copy(zr.at[j - 1], zr.at[j - 1], zr_recv.at[j - 1]).wait()
        total = total + zr[j - 1].astype(F32)

    def gather_start(buf, sems):
        send_sem, z_recv, xy_recv = sems
        first = buf.at[mine]

        def send(i, _):
            pltpu.make_async_remote_copy(
                src_ref=first, dst_ref=first, send_sem=send_sem, recv_sem=xy_recv,
                device_id=beyond(7 - i), device_id_type=MESH,
            ).start()
            return 0

        for j in (2, 1):
            pltpu.make_async_remote_copy(
                src_ref=first, dst_ref=first, send_sem=send_sem, recv_sem=z_recv.at[j - 1],
                device_id=along(j), device_id_type=MESH,
            ).start()
        lax.fori_loop(0, 8, send, 0)
        relay(buf, mine, sems)

    def relay(buf, owner, sems):
        send_sem, _, xy_recv = sems
        piece = buf.at[owner]

        def send(i, _):
            pltpu.make_async_remote_copy(
                src_ref=piece, dst_ref=piece, send_sem=send_sem, recv_sem=xy_recv,
                device_id=across(8 - i), device_id_type=MESH,
            ).start()
            return 0

        lax.fori_loop(1, 8, send, 0)

    def gather_finish(buf, sems):
        _, z_recv, xy_recv = sems
        for j in (1, 2):
            owner = lax.div(source(j), 2) * 8 + xy
            pltpu.make_async_copy(buf.at[owner], buf.at[owner], z_recv.at[j - 1]).wait()
            relay(buf, owner, sems)
        pieces = buf.at[pl.ds(0, 29)]
        pltpu.make_async_copy(pieces, pieces, xy_recv).wait()

    ag1[mine] = total.astype(BF16)
    sems1 = (ag1_send, ag1_z, ag1_recv)
    gather_start(ag1, sems1)
    high = cinv[...].astype(BF16)
    low = (cinv[...] - high.astype(F32)).astype(BF16)
    gather_finish(ag1, sems1)
    residual = ag1[...].reshape(QUARTER, RHS)
    part[...] = (mm(high, residual) + mm(low, residual)).astype(BF16).reshape(2, PIECE, RHS)

    def part_copy(k, e):
        return pltpu.make_async_remote_copy(
            src_ref=part.at[k], dst_ref=pr.at[p], send_sem=pr_send.at[k, e], recv_sem=pr_recv,
            device_id=(2 * odd + k, at(x, z + 8 - sign * e, y)), device_id_type=MESH,
        )

    for k in range(2):
        part_copy(k, 1).start()

        @pl.when(p != 2 * odd + k)
        def _():
            part_copy(k, 0).start()

        @pl.when(p == 2 * odd + k)
        def _():
            pltpu.make_async_copy(part.at[k], pr.at[p], pr_recv).start()

    pltpu.make_async_copy(pr, pr, pr_recv).wait()
    ag2[mine] = (pr[0].astype(F32) + pr[1].astype(F32) + pr[2].astype(F32) + pr[3].astype(F32)).astype(BF16)
    sems2 = (ag2_send, ag2_z, ag2_recv)
    gather_start(ag2, sems2)
    gather_finish(ag2, sems2)
    solved = ag2[...].reshape(QUARTER, RHS)
    for j in (1, 2, 3, 0):
        to = lax.rem(p + j, 4)
        chosen = mm(oh2[pl.ds(pl.multiple_of(to * 128, 128), BOTH), :], solved).astype(BF16)
        if j == 0:
            lr[p] = chosen
        else:
            lp[j] = chosen
            pltpu.make_async_remote_copy(
                src_ref=lp.at[j], dst_ref=lr.at[p], send_sem=lk_send, recv_sem=lk_recv,
                device_id=(to, s), device_id_type=MESH,
            ).start()
    pltpu.make_async_copy(lr.at[pl.ds(0, 3)], lr.at[pl.ds(0, 3)], lk_recv).wait()
    total = lr[0].astype(F32) + lr[1].astype(F32) + lr[2].astype(F32) + lr[3].astype(F32)
    looked[0:BOTH, :] = total.astype(BF16)

    exchange(1)

    for l in range(2):
        for m in range(3):
            rows = slice(m * FACE, (m + 1) * FACE)
            own[l, :, rows] = mm(pt[l, rows, :], w[1, l].reshape(IFACE, RHS)).T.astype(BF16)
            acc[l, rows, :] = mm(pt[l, rows, 0:FACE], w[1, 1 - l, 0])
    for l in range(2):
        arrived(1, l)
        for m in range(3):
            other[l, :, m * FACE : (m + 1) * FACE] = permuted(1, l, m).T.astype(BF16)

    for one in face_copies:
        one.wait_send()
    pltpu.make_async_copy(pm_all.at[pl.ds(0, 7)], pm_all.at[pl.ds(0, 7)], pm_send).wait()
    for l in range(2):
        pltpu.make_async_copy(halves, halves, con_send.at[l]).wait()
    for buf, sem, count in ((ag1, rs_send, 21), (zr, zr_send, 3), (ag1, ag1_send, 31), (ag2, ag2_send, 31)):
        sent = buf.at[pl.ds(0, count)]
        pltpu.make_async_copy(sent, sent, sem).wait()
    pltpu.make_async_copy(lr.at[pl.ds(0, 3)], lr.at[pl.ds(0, 3)], lk_send).wait()
    for k in range(2):
        part_copy(k, 1).wait_send()

        @pl.when(p != 2 * odd + k)
        def _():
            part_copy(k, 0).wait_send()


def on_device(*operands):
    vmem, dma = pltpu.VMEM, pltpu.SemaphoreType.DMA
    operands = [pltpu.with_memory_space_constraint(one, pltpu.HBM) for one in operands]
    own, other = pl.pallas_call(
        kernel,
        out_shape=[jax.ShapeDtypeStruct((2, RHS, IFACE), BF16)] * 2,
        in_specs=[pl.BlockSpec(memory_space=pl.ANY)] * 8,
        out_specs=[pl.BlockSpec(memory_space=pltpu.VMEM)] * 2,
        scratch_shapes=[
            vmem((2, RHS, IFACE), BF16),
            vmem((2, IFACE, IFACE), BF16),
            vmem((2, 3, FACE, FACE), BF16),
            vmem((2, IFACE, IFACE), BF16),
            vmem((2, PRIM, IFACE), BF16),
            vmem((2, IFACE), I32),
            vmem((2, PRIM), I32),
            vmem((BOTH, QUARTER), F32),
            vmem((2, IFACE, IFACE), BF16),
            vmem((2, IFACE, IFACE), BF16),
            vmem((2, IFACE, IFACE), BF16),
            vmem((2, IFACE, RHS), BF16),
            vmem((2, IFACE, RHS), BF16),
            vmem((2, 2, 3, FACE, RHS), BF16),
            vmem((2, 2, 2, FACE, RHS), BF16),
            vmem((2, IFACE, RHS), F32),
            vmem((2, IFACE, RHS), BF16),
            vmem((2, IFACE, RHS), F32),
            vmem((2, 128, IFACE), F32),
            vmem((2, IFACE, 128), BF16),
            vmem((8, 128), I32),
            vmem((8, 8, 128), I32),
            vmem((8, 128, RHS), BF16),
            vmem((QUARTER, 1024), BF16),
            vmem((512, QUARTER), BF16),
            vmem((3, 8, PIECE, RHS), BF16),
            vmem((3, 8, PIECE, RHS), BF16),
            vmem((2, PIECE, RHS), BF16),
            vmem((3, PIECE, RHS), BF16),
            vmem((OWNERS, PIECE, RHS), BF16),
            vmem((2, PIECE, RHS), BF16),
            vmem((4, PIECE, RHS), BF16),
            vmem((OWNERS, PIECE, RHS), BF16),
            vmem((4, BOTH, RHS), BF16),
            vmem((4, BOTH, RHS), BF16),
            vmem((128, RHS), BF16),
            dma((9,)), dma((2, 2, 2)), dma((2, 2, 2)), dma, dma, dma((2,)), dma((2,)),
            dma, dma((3,)), dma, dma((3,)), dma, dma((3,)), dma, dma((2, 2)), dma, dma, dma((3,)), dma, dma, dma,
        ],
        compiler_params=pltpu.CompilerParams(
            collective_id=0, has_side_effects=True, vmem_limit_bytes=48 * 1024 * 1024
        ),
        cost_estimate=pl.CostEstimate(flops=3_000_000_000, bytes_accessed=9_000_000, transcendentals=0),
    )(*operands)
    return own.astype(F32) + other.astype(F32)


def solution(mesh):
    return jax.shard_map(
        on_device,
        mesh=mesh,
        in_specs=(
            P(("plane", "sub"), None, None),
            P(("plane", "sub"), None, None),
            P(("plane", "sub"), None, None, None),
            P(("plane", "sub"), None, None),
            P(("plane", "sub"), None, None),
            P(("plane", "sub"), None),
            P(("plane", "sub"), None),
            P("sub", None),
        ),
        out_specs=P(("plane", "sub"), None, None),
        check_vma=False,
    )
```

```python
import jax
import jax.numpy as jnp
from jax import lax
from jax.experimental import pallas as pl
from jax.experimental.pallas import tpu as pltpu
from jax.sharding import PartitionSpec as P

MESH = pl.DeviceIdType.MESH
F32, BF16, I32 = jnp.float32, jnp.bfloat16, jnp.int32
RHS, IFACE, FACE, PRIM = 128, 768, 256, 48
BOTH = 2 * PRIM
QUARTER = 1536
OWNERS = 32
PIECE = QUARTER // OWNERS


def mm(a, b):
    return jnp.dot(a, b, preferred_element_type=F32)


def onehot(mask):
    return jnp.where(mask, 1.0, 0.0).astype(BF16)


def column(row):
    return jnp.broadcast_to(row, (128, 128)).T


def kernel(
    res_h, schur_h, finv_h, linv_h, basis_h, fd_h, pm_h, cinv_h, own, other,
    res, schur, finv, linv, basis, fd, pm, cinv,
    pt, pp, sp, img, vec, w, got, acc, avg, loc, bpad, bt,
    pm_row, pm_all, con, oh1, oh2, rpart, rs, zs, zr, ag1, part, pr, ag2, lp, lr, looked,
    load_sem, face_send, face_recv, pm_send, pm_recv, con_send, con_recv,
    rs_send, rs_recv, zr_send, zr_recv, ag1_send, ag1_z, ag1_recv, pr_send, pr_recv,
    ag2_send, ag2_z, ag2_recv, lk_send, lk_recv,
):
    p, s = lax.axis_index("plane"), lax.axis_index("sub")
    x, z, y = lax.div(s, 32), lax.rem(lax.div(s, 4), 8), lax.rem(s, 4)
    pair, odd = lax.div(z, 2), lax.rem(z, 2)
    sign = 2 * odd - 1
    xy = x * 4 + y
    mine = pair * 8 + xy

    def at(ax, az, ay):
        return lax.rem(ax, 2) * 32 + lax.rem(az, 8) * 4 + lax.rem(ay, 4)

    def along(j):
        return p, at(x, z + 8 + sign * j, y)

    def source(j):
        return lax.rem(z + 8 + (sign * j if j % 2 else -sign * j), 8)

    def beyond(i):
        return p, at(x + lax.div(i, 4), z + 8 + 3 * sign, y + lax.rem(i, 4))

    def across(i):
        return p, at(x + lax.div(i, 4), z, y + lax.rem(i, 4))

    def near(j):
        return lax.rem(p + lax.rem(j, 4), 4), at(x, z + 8 - sign * lax.div(j, 4), y)

    up, down = lax.rem(s + 1, 64), lax.rem(s + 63, 64)
    core = p + 1 - 2 * lax.rem(p, 2)
    far = p + 2 - 4 * lax.div(p, 2)

    def load(i, src, dst):
        return pltpu.make_async_copy(src, dst, load_sem.at[i])

    loads = [
        load(0, fd_h, fd),
        load(1, pm_h, pm),
        load(2, res_h, res),
        load(3, schur_h.at[0], schur.at[0]),
        load(4, schur_h.at[1], schur.at[1]),
        load(5, finv_h, finv),
        load(6, basis_h, basis),
        load(7, linv_h, linv),
        load(8, cinv_h.at[:, pl.ds(pl.multiple_of(p * QUARTER, QUARTER), QUARTER)], cinv),
    ]
    for one in loads:
        one.start()

    con[...] = jnp.zeros_like(con)
    looked[...] = jnp.zeros_like(looked)
    barrier = pltpu.get_barrier_semaphore()

    def greet(to):
        pl.semaphore_signal(barrier, inc=1, device_id=to, device_id_type=MESH)

    def greet_across(i, _):
        greet(across(i))
        return 0

    def greet_near(j, _):
        greet(near(j))
        return 0

    def greet_beyond(i, _):
        greet(beyond(i))
        return 0

    for j in (1, 2):
        greet((p, at(x, source(j), y)))
    lax.fori_loop(0, 8, greet_beyond, 0)
    lax.fori_loop(1, 8, greet_across, 0)
    lax.fori_loop(1, 8, greet_near, 0)
    greet((p, up))
    greet((p, down))

    loads[1].wait()
    pm_row[...] = jnp.full((8, 128), -1, I32)
    pm_row[0:2, 0:PRIM] = pm[...]
    first = pm_row[0:1, :]
    second = pltpu.roll(jnp.broadcast_to(pm_row[1:2, :], (8, 128)), PRIM, 1)
    lane = lax.broadcasted_iota(I32, (8, 128), 1)
    pm_row[...] = jnp.where(lane < PRIM, jnp.broadcast_to(first, (8, 128)), jnp.where(lane < BOTH, second, -1))
    slot = odd * 4 + p
    pm_all[slot] = pm_row[...]

    def image(l):
        for m in range(3):
            rows = slice(m * FACE, (m + 1) * FACE)
            img[l, rows, :] = lax.dot_general(
                schur[l, rows, :], res[l], (((1,), (1,)), ((), ())), preferred_element_type=F32
            ).astype(BF16)

    def build_pp(l):
        row = fd[l : l + 1, :].astype(F32)
        for b in range(6):
            col = column(row[:, b * 128 : (b + 1) * 128])
            for c in range(6):
                lanes = lax.broadcasted_iota(I32, (128, 128), 1).astype(F32) + float(c * 128)
                pp[l, b * 128 : (b + 1) * 128, c * 128 : (c + 1) * 128] = onehot(col == lanes)

    def weigh(d, l, k):
        rows = slice(k * FACE, (k + 1) * FACE)
        if d == 0:
            faces = mm(pp[l, rows, :], img[l])
        else:
            faces = mm(sp[l, rows, :], vec[l])
        w[d, l, k] = mm(finv[l, k], faces.astype(BF16)).astype(BF16)

    def prepare(l):
        for k in range(3):
            rows = slice(k * FACE, (k + 1) * FACE)
            sp[l, rows, :] = mm(pp[l, rows, :], schur[l]).astype(BF16)

    def face_copy(d, l, k):
        if k == 1:
            to, there = (p, down if l == 0 else up), 1 - l
        else:
            to, there = (core if l == 0 else far, s), l
        return pltpu.make_async_remote_copy(
            src_ref=w.at[d, l, k],
            dst_ref=got.at[d, there, k - 1],
            send_sem=face_send.at[d, l, k - 1],
            recv_sem=face_recv.at[d, there, k - 1],
            device_id=to,
            device_id_type=MESH,
        )

    def arrived(d, l):
        for k in range(2):
            pltpu.make_async_copy(got.at[d, l, k], got.at[d, l, k], face_recv.at[d, l, k]).wait()

    def permute_own():
        for l in range(2):
            for m in range(3):
                rows = slice(m * FACE, (m + 1) * FACE)
                acc[l, rows, :] = mm(pt[l, rows, :], w[0, l].reshape(IFACE, RHS)) + mm(
                    pt[l, rows, 0:FACE], w[0, 1 - l, 0]
                )

    def permuted(d, l, m):
        rows = slice(m * FACE, (m + 1) * FACE)
        return acc[l, rows, :] + mm(pt[l, rows, FACE:], got[d, l].reshape(2 * FACE, RHS))

    face_copies = []

    def exchange(d):
        for l in range(2):
            if d == 0:
                loads[3 + l].wait()
                image(l)
                build_pp(l)
                if l == 0:
                    loads[5].wait()
            else:
                for m in range(3):
                    rows = slice(m * FACE, (m + 1) * FACE)
                    vec[l, rows, :] = (loc[l, rows, :] + mm(bt[l, rows, :], looked[...])).astype(BF16)
            for k in (1, 2):
                weigh(d, l, k)
                if d == 0 and l == 0 and k == 1:
                    pl.semaphore_wait(barrier, 2 + 8 + 7 + 7 + 2)
                    lax.fori_loop(1, 8, send_pm, 0)
                one = face_copy(d, l, k)
                one.start()
                face_copies.append(one)
        for l in range(2):
            weigh(d, l, 0)

    def send_pm(j, _):
        pltpu.make_async_remote_copy(
            src_ref=pm_row, dst_ref=pm_all.at[slot], send_sem=pm_send, recv_sem=pm_recv,
            device_id=near(j), device_id_type=MESH,
        ).start()
        return 0

    loads[0].wait()
    loads[2].wait()
    exchange(0)

    for l in range(2):
        row = fd[l : l + 1, :].astype(F32)
        for m in range(3):
            rows = lax.broadcasted_iota(I32, (FACE, IFACE), 0).astype(F32) + float(m * FACE)
            pt[l, m * FACE : (m + 1) * FACE, :] = onehot(rows == row)
    permute_own()
    loads[6].wait()
    bpad[...] = jnp.zeros_like(bpad)
    for l in range(2):
        bpad[l, l * PRIM : (l + 1) * PRIM, :] = basis[l].astype(F32)
        for b in range(6):
            bt[l, b * 128 : (b + 1) * 128, :] = bpad[l, :, b * 128 : (b + 1) * 128].T.astype(BF16)
    pltpu.make_async_copy(pm_all.at[pl.ds(0, 7)], pm_all.at[pl.ds(0, 7)], pm_recv).wait()
    for t in range(8):
        row = pm_all[t, 0:1, :].astype(F32) - (p * QUARTER).astype(F32)
        for m in range(6):
            rows = lax.broadcasted_iota(I32, (256, 128), 0).astype(F32) + float(m * 256)
            oh1[m * 256 : (m + 1) * 256, t * 128 : (t + 1) * 128] = onehot(rows == row)

    for l in range(2):
        arrived(0, l)
        for m in range(3):
            avg[l, m * FACE : (m + 1) * FACE, :] = permuted(0, l, m).astype(BF16)
        con[slot, l * PRIM : (l + 1) * PRIM, :] = mm(basis[l], avg[l]).astype(BF16)

        def send_con(j, _, l=l):
            half = con.at[slot, pl.ds(l * PRIM, PRIM)]
            pltpu.make_async_remote_copy(
                src_ref=half, dst_ref=half, send_sem=con_send.at[l], recv_sem=con_recv.at[l],
                device_id=near(8 - j), device_id_type=MESH,
            ).start()
            return 0

        lax.fori_loop(1, 8, send_con, 0)

    loads[7].wait()
    for l in range(2):
        for m in range(3):
            loc[l, m * FACE : (m + 1) * FACE, :] = mm(linv[l, m * FACE : (m + 1) * FACE, :], avg[l])
    prepare(0)
    loads[8].wait()

    halves = con.at[pl.ds(0, 7), pl.ds(0, PRIM)]
    for l in range(2):
        pltpu.make_async_copy(halves, halves, con_recv.at[l]).wait()
    every = con[...].reshape(8 * 128, RHS)
    far_pair = lax.rem(pair + 2, 4)
    next_pair = lax.rem(pair + 4 + sign, 4)
    for n, target in enumerate((far_pair, next_pair, pair)):
        rows = oh1[pl.ds(pl.multiple_of(target * 8 * PIECE, 8 * PIECE), 8 * PIECE), :]
        rpart[n] = mm(rows, every).astype(BF16).reshape(8, PIECE, RHS)

        def send_rs(i, _, n=n):
            to = across(8 - i)
            txy = lax.div(to[1], 32) * 4 + lax.rem(to[1], 4)
            pltpu.make_async_remote_copy(
                src_ref=rpart.at[n, txy], dst_ref=rs.at[n, xy], send_sem=rs_send, recv_sem=rs_recv.at[n],
                device_id=to, device_id_type=MESH,
            ).start()
            return 0

        lax.fori_loop(1, 8, send_rs, 0)
        rs[n, xy] = rpart[n, xy]

    for q in range(4):
        c = pm_all[odd * 4 + q].astype(F32)
        block = jnp.floor((c + 0.5) * (1.0 / 96.0))
        rem = c - 96.0 * block
        cx = jnp.floor((block + 0.5) * (1.0 / 32.0))
        cz = jnp.floor((block - 32.0 * cx + 0.5) * 0.25)
        cy = block - 32.0 * cx - 4.0 * cz
        cg = jnp.floor((cz + 0.5) * 0.5)
        ck = jnp.floor((rem + 0.5) * (1.0 / 48.0))
        owner = cg * 8.0 + cx * 4.0 + cy
        code = (2.0 * (cz - 2.0 * cg) + ck) * float(QUARTER) + owner * float(PIECE) + rem - 48.0 * ck
        code = jnp.where(c < 0.0, -1.0, code) - (p * QUARTER).astype(F32)
        col = column(code[0:1, :])
        for b in range(QUARTER // 128):
            lanes = lax.broadcasted_iota(I32, (128, 128), 1).astype(F32) + float(b * 128)
            oh2[q * 128 : (q + 1) * 128, b * 128 : (b + 1) * 128] = onehot(col == lanes)

    prepare(1)

    def z_copy(src, j, n):
        return pltpu.make_async_remote_copy(
            src_ref=src, dst_ref=zr.at[j - 1], send_sem=zr_send, recv_sem=zr_recv.at[j - 1],
            device_id=along(j), device_id_type=MESH,
        )

    for n in range(3):
        seven = rs.at[n, pl.ds(0, 7)]
        pltpu.make_async_copy(seven, seven, rs_recv.at[n]).wait()
        total = rs[n, 0].astype(F32)
        for i in range(1, 8):
            total = total + rs[n, i].astype(F32)
        if n < 2:
            zs[n] = total.astype(BF16)
            for j in ((3,), (2, 1))[n]:
                z_copy(zs.at[n], j, n).start()
    for j in (1, 2, 3):
        pltpu.make_async_copy(zr.at[j - 1], zr.at[j - 1], zr_recv.at[j - 1]).wait()
        total = total + zr[j - 1].astype(F32)

    def gather_start(buf, sems):
        send_sem, z_recv, xy_recv = sems
        first = buf.at[mine]

        def send(i, _):
            pltpu.make_async_remote_copy(
                src_ref=first, dst_ref=first, send_sem=send_sem, recv_sem=xy_recv,
                device_id=beyond(7 - i), device_id_type=MESH,
            ).start()
            return 0

        for j in (2, 1):
            pltpu.make_async_remote_copy(
                src_ref=first, dst_ref=first, send_sem=send_sem, recv_sem=z_recv.at[j - 1],
                device_id=along(j), device_id_type=MESH,
            ).start()
        lax.fori_loop(0, 8, send, 0)
        relay(buf, mine, sems)

    def relay(buf, owner, sems):
        send_sem, _, xy_recv = sems
        piece = buf.at[owner]

        def send(i, _):
            pltpu.make_async_remote_copy(
                src_ref=piece, dst_ref=piece, send_sem=send_sem, recv_sem=xy_recv,
                device_id=across(8 - i), device_id_type=MESH,
            ).start()
            return 0

        lax.fori_loop(1, 8, send, 0)

    def gather_finish(buf, sems):
        _, z_recv, xy_recv = sems
        for j in (1, 2):
            owner = lax.div(source(j), 2) * 8 + xy
            pltpu.make_async_copy(buf.at[owner], buf.at[owner], z_recv.at[j - 1]).wait()
            relay(buf, owner, sems)
        pieces = buf.at[pl.ds(0, 29)]
        pltpu.make_async_copy(pieces, pieces, xy_recv).wait()

    ag1[mine] = total.astype(BF16)
    sems1 = (ag1_send, ag1_z, ag1_recv)
    gather_start(ag1, sems1)
    high = cinv[...].astype(BF16)
    low = (cinv[...] - high.astype(F32)).astype(BF16)
    gather_finish(ag1, sems1)
    residual = ag1[...].reshape(QUARTER, RHS)

    def part_copy(k, e):
        return pltpu.make_async_remote_copy(
            src_ref=part.at[k], dst_ref=pr.at[p], send_sem=pr_send.at[k, e], recv_sem=pr_recv,
            device_id=(2 * odd + k, at(x, z + 8 - sign * e, y)), device_id_type=MESH,
        )

    for k in range(2):
        rows = slice(k * PIECE, (k + 1) * PIECE)
        part[k] = (mm(high[rows], residual) + mm(low[rows], residual)).astype(BF16)
        part_copy(k, 1).start()

        @pl.when(p != 2 * odd + k)
        def _():
            part_copy(k, 0).start()

        @pl.when(p == 2 * odd + k)
        def _():
            pltpu.make_async_copy(part.at[k], pr.at[p], pr_recv).start()

    pltpu.make_async_copy(pr, pr, pr_recv).wait()
    ag2[mine] = (pr[0].astype(F32) + pr[1].astype(F32) + pr[2].astype(F32) + pr[3].astype(F32)).astype(BF16)
    sems2 = (ag2_send, ag2_z, ag2_recv)
    gather_start(ag2, sems2)
    gather_finish(ag2, sems2)
    solved = ag2[...].reshape(QUARTER, RHS)
    for j in (1, 2, 3, 0):
        to = lax.rem(p + j, 4)
        chosen = mm(oh2[pl.ds(pl.multiple_of(to * 128, 128), BOTH), :], solved).astype(BF16)
        if j == 0:
            lr[p] = chosen
        else:
            lp[j] = chosen
            pltpu.make_async_remote_copy(
                src_ref=lp.at[j], dst_ref=lr.at[p], send_sem=lk_send, recv_sem=lk_recv,
                device_id=(to, s), device_id_type=MESH,
            ).start()
    pltpu.make_async_copy(lr.at[pl.ds(0, 3)], lr.at[pl.ds(0, 3)], lk_recv).wait()
    total = lr[0].astype(F32) + lr[1].astype(F32) + lr[2].astype(F32) + lr[3].astype(F32)
    looked[0:BOTH, :] = total.astype(BF16)

    exchange(1)

    for l in range(2):
        for m in range(3):
            rows = slice(m * FACE, (m + 1) * FACE)
            own[l, :, rows] = mm(pt[l, rows, :], w[1, l].reshape(IFACE, RHS)).T.astype(BF16)
            acc[l, rows, :] = mm(pt[l, rows, 0:FACE], w[1, 1 - l, 0])
    for l in range(2):
        arrived(1, l)
        for m in range(3):
            other[l, :, m * FACE : (m + 1) * FACE] = permuted(1, l, m).T.astype(BF16)

    for one in face_copies:
        one.wait_send()
    pltpu.make_async_copy(pm_all.at[pl.ds(0, 7)], pm_all.at[pl.ds(0, 7)], pm_send).wait()
    for l in range(2):
        pltpu.make_async_copy(halves, halves, con_send.at[l]).wait()
    for buf, sem, count in ((ag1, rs_send, 21), (zr, zr_send, 3), (ag1, ag1_send, 31), (ag2, ag2_send, 31)):
        sent = buf.at[pl.ds(0, count)]
        pltpu.make_async_copy(sent, sent, sem).wait()
    pltpu.make_async_copy(lr.at[pl.ds(0, 3)], lr.at[pl.ds(0, 3)], lk_send).wait()
    for k in range(2):
        part_copy(k, 1).wait_send()

        @pl.when(p != 2 * odd + k)
        def _():
            part_copy(k, 0).wait_send()


def on_device(*operands):
    vmem, dma = pltpu.VMEM, pltpu.SemaphoreType.DMA
    operands = [pltpu.with_memory_space_constraint(one, pltpu.HBM) for one in operands]
    own, other = pl.pallas_call(
        kernel,
        out_shape=[jax.ShapeDtypeStruct((2, RHS, IFACE), BF16)] * 2,
        in_specs=[pl.BlockSpec(memory_space=pl.ANY)] * 8,
        out_specs=[pl.BlockSpec(memory_space=pltpu.VMEM)] * 2,
        scratch_shapes=[
            vmem((2, RHS, IFACE), BF16),
            vmem((2, IFACE, IFACE), BF16),
            vmem((2, 3, FACE, FACE), BF16),
            vmem((2, IFACE, IFACE), BF16),
            vmem((2, PRIM, IFACE), BF16),
            vmem((2, IFACE), I32),
            vmem((2, PRIM), I32),
            vmem((BOTH, QUARTER), F32),
            vmem((2, IFACE, IFACE), BF16),
            vmem((2, IFACE, IFACE), BF16),
            vmem((2, IFACE, IFACE), BF16),
            vmem((2, IFACE, RHS), BF16),
            vmem((2, IFACE, RHS), BF16),
            vmem((2, 2, 3, FACE, RHS), BF16),
            vmem((2, 2, 2, FACE, RHS), BF16),
            vmem((2, IFACE, RHS), F32),
            vmem((2, IFACE, RHS), BF16),
            vmem((2, IFACE, RHS), F32),
            vmem((2, 128, IFACE), F32),
            vmem((2, IFACE, 128), BF16),
            vmem((8, 128), I32),
            vmem((8, 8, 128), I32),
            vmem((8, 128, RHS), BF16),
            vmem((QUARTER, 1024), BF16),
            vmem((512, QUARTER), BF16),
            vmem((3, 8, PIECE, RHS), BF16),
            vmem((3, 8, PIECE, RHS), BF16),
            vmem((2, PIECE, RHS), BF16),
            vmem((3, PIECE, RHS), BF16),
            vmem((OWNERS, PIECE, RHS), BF16),
            vmem((2, PIECE, RHS), BF16),
            vmem((4, PIECE, RHS), BF16),
            vmem((OWNERS, PIECE, RHS), BF16),
            vmem((4, BOTH, RHS), BF16),
            vmem((4, BOTH, RHS), BF16),
            vmem((128, RHS), BF16),
            dma((9,)), dma((2, 2, 2)), dma((2, 2, 2)), dma, dma, dma((2,)), dma((2,)),
            dma, dma((3,)), dma, dma((3,)), dma, dma((3,)), dma, dma((2, 2)), dma, dma, dma((3,)), dma, dma, dma,
        ],
        compiler_params=pltpu.CompilerParams(
            collective_id=0, has_side_effects=True, vmem_limit_bytes=48 * 1024 * 1024
        ),
        cost_estimate=pl.CostEstimate(flops=3_000_000_000, bytes_accessed=9_000_000, transcendentals=0),
    )(*operands)
    return own.astype(F32) + other.astype(F32)


def solution(mesh):
    return jax.shard_map(
        on_device,
        mesh=mesh,
        in_specs=(
            P(("plane", "sub"), None, None),
            P(("plane", "sub"), None, None),
            P(("plane", "sub"), None, None, None),
            P(("plane", "sub"), None, None),
            P(("plane", "sub"), None, None),
            P(("plane", "sub"), None),
            P(("plane", "sub"), None),
            P("sub", None),
        ),
        out_specs=P(("plane", "sub"), None, None),
        check_vma=False,
    )
```
